32 devices in a mesh: vv: 8 (over y, x, core), oo: 4 (over z).
Axes of the slice: x: 2, y: 2, z: 4, core: 2. Of those that a mesh axis runs over, the one named last changes fastest.
Arguments:
- amplitudes: bfloat16 [24, 512, 128], P('vv', 'oo'), may hold values from -6 to 6
- tile_counts: int32 [24], P('vv'), may hold values from 1 to 48, as said below
- tile_lists: int32 [24, 48], P('vv', 'oo'), may hold values from 0 to 23, as said below
- integrals: bfloat16 [24, 48, 128, 128], P('vv', 'oo'), may hold values from -0.078125 to 0.078125
Outputs:
- ladder: float32 [512, 3072], P('oo', 'vv')
The draws below stay inside these ranges and needn't reach their ends.
Inputs may be any that keep to these rules, and one draw needn't show every extreme that they name: `tile_counts`: every tile's list has at least one live slot, and some tile's list is full. `tile_lists`: a list may name a tile more than once; slots at or after the row's count name tiles too but are not live.
All inputs are finite; a program needn't handle non-finite values.
Results may differ from the reference program's by a relative error of at most 0.0003.
Values may be sent and summed in bfloat16 or wider, within the bound.
No kernel may reach another device: no remote copies, remote signals or barrier semaphores. Data moves between devices by JAX's collectives and lax.ppermute only.
A program may use at most 64 MiB of HBM per device.

```python
import jax
import jax.numpy as jnp
from jax import lax

TILE = 128
OCC_PAIRS = 512
NT = 24
LIST = 48


def draw_tile_counts(key, part):
    key = jax.random.fold_in(key, 11)
    first, second, third = jax.random.split(key, 3)
    heavy = jax.random.randint(first, (NT,), 0, 4) == 0
    high = LIST - jax.random.randint(second, (NT,), 0, max(LIST // 8, 1))
    light = jax.random.randint(third, (NT,), 1, max(LIST // 3, 1) + 1)
    counts = jnp.where(heavy, high, light).astype(jnp.int32)
    return counts.at[0].set(LIST)


def draw_tile_lists(key, part):
    key = jax.random.fold_in(key, 23)
    lists = jax.random.randint(key, (NT, LIST), 0, NT).astype(jnp.int32)
    lists = lists.at[0, 0].set(NT - 1)
    return lists.at[NT - 1, 0].set(0)


def steps_of(key, dims, cuts, least, top_value):
    factor_of, own = 1.0, jax.random.fold_in(key, 6)
    for position, shards_of in cuts:
        draws = jnp.exp(jax.random.uniform(jax.random.fold_in(own, position), (shards_of,), jnp.float32, least / len(cuts), top_value / len(cuts)))
        factor_of = factor_of * jnp.repeat(draws, dims[position] // shards_of).reshape([-1 if axis == position else 1 for axis in range(len(dims))])
    return factor_of


def noise(key, shape, scale, reach, shards=(), kind=jnp.bfloat16):
    array = jax.random.normal(key, shape, jnp.float32) * scale
    if len(shards) > 0:
        array = steps_of(key, shape, shards, -0.22, 0.18) * array
    return jnp.clip(array, min=-reach, max=reach).astype(kind)


def setup_inputs(seed: int = 0) -> dict:
    arg_keys = jax.random.split(jax.random.key(seed), 5)
    amplitudes = noise(arg_keys[0], (NT, OCC_PAIRS, TILE), 1.0, 6.0, ((0, 8), (1, 4)))
    tile_counts = draw_tile_counts(jax.random.fold_in(arg_keys[4], 71), 0)
    tile_lists = draw_tile_lists(jax.random.fold_in(arg_keys[4], 71), 0)
    integrals = noise(arg_keys[3], (NT, LIST, TILE, TILE), (TILE * LIST) ** -0.5, 0.078125, ((0, 8), (1, 4)))
    return {"amplitudes": amplitudes, "tile_counts": tile_counts, "tile_lists": tile_lists, "integrals": integrals}


def one_tile(amplitudes, row_list, row_count, row_integrals):
    picked = jnp.take(amplitudes, row_list, axis=0)
    slot_ids = jnp.arange(row_list.shape[0], dtype=jnp.int32)
    living = slot_ids < row_count
    picked = jnp.where(living[:, None, None], picked, jnp.zeros_like(picked))
    return jnp.einsum("lpc,lqc->pq", picked.astype(jnp.float32), row_integrals.astype(jnp.float32))


def reference(amplitudes, tile_counts, tile_lists, integrals):
    def handle(packed):
        row_list, row_count, row_integrals = packed
        return one_tile(amplitudes, row_list, row_count, row_integrals)

    tiles = lax.map(handle, (tile_lists, tile_counts, integrals))
    return jnp.transpose(tiles, (1, 0, 2)).reshape(tiles.shape[1], tiles.shape[0] * tiles.shape[2])
```

```python
import jax
import jax.numpy as jnp
from jax import lax
from jax.experimental import pallas as pl
from jax.experimental.pallas import tpu as pltpu
from jax.sharding import PartitionSpec as P

VMEM_BYTES = 48 * 1024 * 1024


def shift(value, axis, size, mask):
    return lax.ppermute(value, axis, [(j, j ^ mask) for j in range(size)])


def contract(lists_ref, live_ref, stage, integrals_ref, out_ref):
    tile_dev, slots, width, depth = integrals_ref.shape
    blocks, _, rows, _ = stage.shape
    dims = (((1,), (1,)), ((), ()))
    for a in range(tile_dev):
        live = live_ref[a]

        def step(pair, total, a=a, live=live):
            s = 2 * pair
            left = stage[:, lists_ref[a, s]].reshape(blocks * rows, depth)
            right = stage[:, lists_ref[a, jnp.minimum(s + 1, slots - 1)]].reshape(blocks * rows, depth)
            second = jnp.where(s + 1 < live, integrals_ref[a, jnp.minimum(s + 1, slots - 1)], jnp.zeros((width, depth), integrals_ref.dtype))
            both = jnp.concatenate([left, right], axis=1)
            weights = jnp.concatenate([integrals_ref[a, s], second], axis=1)
            return total + lax.dot_general(both, weights, dims, preferred_element_type=jnp.float32)

        total = lax.fori_loop(0, (live + 1) // 2, step, jnp.zeros((blocks * rows, width), jnp.float32))
        for k in range(blocks):
            out_ref[k, :, a * width:(a + 1) * width] = total[k * rows:(k + 1) * rows]


def ladder_kernel(lists_ref, live_ref, place_ref, *refs, layout):
    count = len(layout)
    pieces, integrals_ref, out_ref, stage, sems = refs[:count], refs[count], refs[count + 1], refs[count + 2], refs[count + 3]
    copies = []
    for n, (mask, first) in enumerate(layout):
        piece = pieces[n]
        base = (place_ref[0] ^ mask) * piece.shape[1]
        copy = pltpu.make_async_copy(
            piece, stage.at[pl.ds(first, piece.shape[0]), pl.ds(base, piece.shape[1])], sems.at[n]
        )
        copy.start()
        copies.append(copy)
    for copy in copies:
        copy.wait()
    contract(lists_ref, live_ref, stage, integrals_ref, out_ref)


def partials(lists, live, place, pieces, layout, integrals, blocks, tiles):
    tile_dev, _, width, depth = integrals.shape
    rows = pieces[0].shape[2]
    smem = pl.BlockSpec(memory_space=pltpu.SMEM)
    return pl.pallas_call(
        lambda *refs: ladder_kernel(*refs, layout=layout),
        out_shape=jax.ShapeDtypeStruct((blocks, rows, tile_dev * width), jnp.float32),
        in_specs=[smem] * 3 + [pl.BlockSpec(memory_space=pl.ANY)] * len(pieces) + [pl.BlockSpec(memory_space=pltpu.VMEM)],
        out_specs=pl.BlockSpec(memory_space=pltpu.VMEM),
        scratch_shapes=[
            pltpu.VMEM((blocks, tiles, rows, depth), integrals.dtype),
            pltpu.SemaphoreType.DMA((len(pieces),)),
        ],
        compiler_params=pltpu.CompilerParams(vmem_limit_bytes=VMEM_BYTES),
    )(lists, live, place, *pieces, integrals)


def on_device(amplitudes, tile_counts, tile_lists, integrals, n_vv, n_oo):
    slots = tile_lists.shape[1]
    tiles = n_vv * amplitudes.shape[0]
    group = lax.axis_index("oo")
    live = jnp.clip(tile_counts - group * slots, 0, slots)
    if (n_vv, n_oo) == (8, 4):
        far = [shift(amplitudes, "oo", n_oo, k) for k in (2, 3)]
        near = shift(amplitudes, "oo", n_oo, 1)
        own = jnp.stack([amplitudes, near] + far)
        by_x = shift(own, "vv", n_vv, 2)
        by_y = shift(own, "vv", n_vv, 4)
        low = shift(by_x[:2], "vv", n_vv, 4)
        high = shift(by_y[2:], "vv", n_vv, 2)
        pieces = [own, by_x, by_y, low, high]
        layout = [(0, 0), (2, 0), (4, 0), (6, 0), (6, 2)]
        pieces = pieces + [shift(p, "vv", n_vv, 1) for p in pieces]
        layout = layout + [(m ^ 1, f) for m, f in layout]
        place = lax.axis_index("vv").astype(jnp.int32).reshape(1)
        parts = partials(tile_lists, live, place, pieces, layout, integrals, n_oo, tiles)
        total = parts[0]
        for k in (2, 3, 1):
            total = total + shift(parts[k], "oo", n_oo, k)
        return total
    rows = lax.all_gather(amplitudes, "oo", axis=0, tiled=False)
    everything = lax.all_gather(rows, "vv", axis=1, tiled=True)
    place = jnp.zeros((1,), jnp.int32)
    parts = partials(tile_lists, live, place, [everything], [(0, 0)], integrals, n_oo, tiles)
    return lax.psum_scatter(parts.reshape(-1, parts.shape[2]), "oo", scatter_dimension=0, tiled=True)


def solution(mesh):
    n_vv, n_oo = mesh.shape["vv"], mesh.shape["oo"]
    placed = (P("vv", "oo", None), P("vv"), P("vv", "oo"), P("vv", "oo", None, None))
    return jax.shard_map(
        lambda *args: on_device(*args, n_vv, n_oo),
        mesh=mesh, in_specs=placed, out_specs=P("oo", "vv"), check_vma=False,
    )
```

```python
import jax
import jax.numpy as jnp
from jax import lax
from jax.experimental import pallas as pl
from jax.experimental.pallas import tpu as pltpu
from jax.sharding import PartitionSpec as P

VMEM_BYTES = 48 * 1024 * 1024
UNROLL = 4
OWN_FLOPS = 4000000000
SMEM = pl.BlockSpec(memory_space=pltpu.SMEM)
VMEM = pl.BlockSpec(memory_space=pltpu.VMEM)
ANY = pl.BlockSpec(memory_space=pl.ANY)


def shift(value, axis, size, mask):
    return lax.ppermute(value, axis, [(j, j ^ mask) for j in range(size)])


def contract(total, lists_ref, a, live, stage, blocks_of):
    blocks, _, rows, depth = stage.shape
    slots = lists_ref.shape[1]
    dims = (((1,), (1,)), ((), ()))

    def pair(s):
        sides, weights = [], []
        for slot in (s, s + 1):
            safe = jnp.minimum(slot, slots - 1)
            block = blocks_of(safe)
            sides.append(stage[:, lists_ref[a, safe]].reshape(blocks * rows, depth))
            weights.append(jnp.where(slot < live, block, jnp.zeros_like(block)))
        return lax.dot_general(
            jnp.concatenate(sides, axis=1), jnp.concatenate(weights, axis=1), dims, preferred_element_type=jnp.float32
        )

    def step(group, total):
        for offset in range(0, UNROLL, 2):
            total = total + pair(UNROLL * group + offset)
        return total

    return lax.fori_loop(0, (live + UNROLL - 1) // UNROLL, step, total)


def gather_pieces(place_ref, pieces, layout, stage, sems):
    copies = []
    for n, (mask, first) in enumerate(layout):
        piece = pieces[n]
        base = (place_ref[0] ^ mask) * piece.shape[1]
        copy = pltpu.make_async_copy(
            piece, stage.at[pl.ds(first, piece.shape[0]), pl.ds(base, piece.shape[1])], sems.at[n]
        )
        copy.start()
        copies.append(copy)
    for copy in copies:
        copy.wait()


def plain_kernel(lists_ref, live_ref, place_ref, piece, integrals_ref, out_ref, stage, sems):
    gather_pieces(place_ref, [piece], [(0, 0)], stage, sems)
    tile_dev, _, width, _ = integrals_ref.shape
    blocks, _, rows, _ = stage.shape
    for a in range(tile_dev):
        zero = jnp.zeros((blocks * rows, width), jnp.float32)
        total = contract(zero, lists_ref, a, live_ref[a], stage, lambda s, a=a: integrals_ref[a, s])
        for k in range(blocks):
            out_ref[k, :, a * width:(a + 1) * width] = total[k * rows:(k + 1) * rows]


def plain_partials(lists, live, everything, integrals):
    blocks, tiles, rows, depth = everything.shape
    tile_dev, _, width, _ = integrals.shape
    return pl.pallas_call(
        plain_kernel,
        out_shape=jax.ShapeDtypeStruct((blocks, rows, tile_dev * width), jnp.float32),
        in_specs=[SMEM] * 3 + [ANY, VMEM],
        out_specs=VMEM,
        scratch_shapes=[pltpu.VMEM((blocks, tiles, rows, depth), everything.dtype), pltpu.SemaphoreType.DMA((1,))],
        compiler_params=pltpu.CompilerParams(vmem_limit_bytes=VMEM_BYTES),
    )(lists, live, jnp.zeros((1,), jnp.int32), everything, integrals)


def cut_kernel(whole, head, tail, sems):
    copies = [
        pltpu.make_async_copy(whole.at[pl.ds(0, head.shape[0])], head, sems.at[0]),
        pltpu.make_async_copy(whole.at[pl.ds(head.shape[0], tail.shape[0])], tail, sems.at[1]),
    ]
    for copy in copies:
        copy.start()
    for copy in copies:
        copy.wait()


def cut(whole, first):
    count = whole.shape[0]
    return pl.pallas_call(
        cut_kernel,
        out_shape=tuple(jax.ShapeDtypeStruct((n,) + whole.shape[1:], whole.dtype) for n in (first, count - first)),
        in_specs=[ANY],
        out_specs=(VMEM,) * 2,
        scratch_shapes=[pltpu.SemaphoreType.DMA((2,))],
        compiler_params=pltpu.CompilerParams(vmem_limit_bytes=VMEM_BYTES),
    )(whole)


def live_slots(counts_ref, a, group, slots):
    return jnp.clip(counts_ref[a] - group * slots, 0, slots)


def own_kernel(layout, counts_ref, lists_ref, place_ref, *refs):
    count = len(layout)
    pieces, integrals_ref = refs[:count], refs[count]
    sums_ref, stage, sems = refs[count + 1:]
    gather_pieces(place_ref, pieces, layout, stage, sems)
    tile_dev, slots, width, _ = integrals_ref.shape
    blocks, _, rows, _ = stage.shape
    for a in range(tile_dev):
        total = jnp.zeros((blocks * rows, width), jnp.float32)
        live = live_slots(counts_ref, a, place_ref[1], slots)
        sums_ref[a] = contract(total, lists_ref, a, live, stage, lambda s, a=a: integrals_ref[a, s])


def other_kernel(first, counts_ref, other_ref, place_ref, stage, sums_ref, others, own_ref, far_ref):
    rows = own_ref.shape[0]
    count, slots, width, _ = others.shape
    for n in range(count):
        live = live_slots(counts_ref, first + n, place_ref[1] ^ 1, slots)
        total = contract(sums_ref[first + n], other_ref, first + n, live, stage, lambda s, n=n: others[n, s])
        own_ref[:, n * width:(n + 1) * width] = total[:rows]
        far_ref[:, n * width:(n + 1) * width] = total[rows:]


def on_pairs(amplitudes, tile_counts, tile_lists, integrals, n_vv, n_oo):
    tile_dev, slots, width, depth = integrals.shape
    rows = amplitudes.shape[1]
    tiles = n_vv * tile_dev
    ready = tile_dev - 1
    place = jnp.stack([lax.axis_index("vv"), lax.axis_index("oo")]).astype(jnp.int32)

    far = shift(amplitudes, "oo", n_oo, 2)
    head, tail = (shift(part, "oo", n_oo, 1) for part in cut(integrals, ready))
    far, amplitudes, sent = lax.optimization_barrier((far, amplitudes, tile_lists))
    other_lists = shift(sent, "oo", n_oo, 1)
    pieces, layout = [], []
    for first, block in enumerate((amplitudes[None], far[None])):
        for mask in (0, 2, 4, 6):
            piece = shift(block, "vv", n_vv, mask) if mask else block
            pieces += [piece, shift(piece, "vv", n_vv, 1)]
            layout += [(mask, first), (mask ^ 1, first)]
    params = pltpu.CompilerParams(vmem_limit_bytes=VMEM_BYTES)
    sums, stage = pl.pallas_call(
        lambda *refs: own_kernel(layout, *refs),
        out_shape=(
            jax.ShapeDtypeStruct((tile_dev, 2 * rows, width), jnp.float32),
            jax.ShapeDtypeStruct((2, tiles, rows, depth), amplitudes.dtype),
        ),
        in_specs=[SMEM] * 3 + [ANY] * len(pieces) + [VMEM],
        out_specs=(VMEM,) * 2,
        scratch_shapes=[pltpu.SemaphoreType.DMA((len(pieces),))],
        compiler_params=params,
        cost_estimate=pl.CostEstimate(flops=OWN_FLOPS, bytes_accessed=2**22, transcendentals=0),
    )(tile_counts, tile_lists, place, *pieces, integrals)
    results = []
    for first, others in ((0, head), (ready, tail)):
        part = jax.ShapeDtypeStruct((rows, others.shape[0] * width), jnp.float32)
        own, away = pl.pallas_call(
            lambda *refs, first=first: other_kernel(first, *refs),
            out_shape=(part,) * 2,
            in_specs=[SMEM] * 3 + [VMEM] * 3,
            out_specs=(VMEM,) * 2,
            compiler_params=params,
            cost_estimate=pl.CostEstimate(flops=2**28, bytes_accessed=2**21, transcendentals=0),
        )(tile_counts, other_lists, place, stage, sums, others)
        results.append(own + shift(away, "oo", n_oo, 2))
    return jnp.concatenate(results, axis=1)


def on_device(amplitudes, tile_counts, tile_lists, integrals, n_vv, n_oo):
    if (n_vv, n_oo) == (8, 4):
        return on_pairs(amplitudes, tile_counts, tile_lists, integrals, n_vv, n_oo)
    slots = tile_lists.shape[1]
    live = jnp.clip(tile_counts - lax.axis_index("oo") * slots, 0, slots)
    rows = lax.all_gather(amplitudes, "oo", axis=0, tiled=False)
    everything = lax.all_gather(rows, "vv", axis=1, tiled=True)
    parts = plain_partials(tile_lists, live, everything, integrals)
    return lax.psum_scatter(parts.reshape(-1, parts.shape[2]), "oo", scatter_dimension=0, tiled=True)


def solution(mesh):
    n_vv, n_oo = mesh.shape["vv"], mesh.shape["oo"]
    placed = (P("vv", "oo", None), P("vv"), P("vv", "oo"), P("vv", "oo", None, None))
    return jax.shard_map(
        lambda *args: on_device(*args, n_vv, n_oo),
        mesh=mesh, in_specs=placed, out_specs=P("oo", "vv"), check_vma=False,
    )
```

```python
import jax
import jax.numpy as jnp
from jax import lax
from jax.experimental import pallas as pl
from jax.experimental.pallas import tpu as pltpu
from jax.sharding import PartitionSpec as P

VMEM_BYTES = 48 * 1024 * 1024
UNROLL = 4
OWN_FLOPS = 4000000000
HEAD_FLOPS = 250000000
TABLE_ROWS = 16
SMEM = pl.BlockSpec(memory_space=pltpu.SMEM)
VMEM = pl.BlockSpec(memory_space=pltpu.VMEM)
ANY = pl.BlockSpec(memory_space=pl.ANY)
HBM = pl.BlockSpec(memory_space=pltpu.HBM)


def shift(value, axis, size, mask):
    return lax.ppermute(value, axis, [(j, j ^ mask) for j in range(size)])


def contract(total, lists_ref, a, live, slots, stage, blocks_of):
    blocks, _, rows, depth = stage.shape
    dims = (((1,), (1,)), ((), ()))

    def pair(s):
        sides, weights = [], []
        for slot in (s, s + 1):
            safe = jnp.minimum(slot, slots - 1)
            block = blocks_of(safe)
            sides.append(stage[:, lists_ref[a, safe]].reshape(blocks * rows, depth))
            weights.append(jnp.where(slot < live, block, jnp.zeros_like(block)))
        return lax.dot_general(
            jnp.concatenate(sides, axis=1), jnp.concatenate(weights, axis=1), dims, preferred_element_type=jnp.float32
        )

    def step(group, total):
        for offset in range(0, UNROLL, 2):
            total = total + pair(UNROLL * group + offset)
        return total

    return lax.fori_loop(0, (live + UNROLL - 1) // UNROLL, step, total)


def gather_pieces(place_ref, pieces, layout, stage, sems):
    copies = []
    for n, (mask, first) in enumerate(layout):
        piece = pieces[n]
        base = (place_ref[0] ^ mask) * piece.shape[1]
        copy = pltpu.make_async_copy(
            piece, stage.at[pl.ds(first, piece.shape[0]), pl.ds(base, piece.shape[1])], sems.at[n]
        )
        copy.start()
        copies.append(copy)
    for copy in copies:
        copy.wait()


def plain_kernel(lists_ref, live_ref, place_ref, piece, integrals_ref, out_ref, stage, sems):
    gather_pieces(place_ref, [piece], [(0, 0)], stage, sems)
    tile_dev, _, width, _ = integrals_ref.shape
    blocks, _, rows, _ = stage.shape
    for a in range(tile_dev):
        zero = jnp.zeros((blocks * rows, width), jnp.float32)
        total = contract(zero, lists_ref, a, live_ref[a], lists_ref.shape[1], stage, lambda s, a=a: integrals_ref[a, s])
        for k in range(blocks):
            out_ref[k, :, a * width:(a + 1) * width] = total[k * rows:(k + 1) * rows]


def plain_partials(lists, live, everything, integrals):
    blocks, tiles, rows, depth = everything.shape
    tile_dev, _, width, _ = integrals.shape
    return pl.pallas_call(
        plain_kernel,
        out_shape=jax.ShapeDtypeStruct((blocks, rows, tile_dev * width), jnp.float32),
        in_specs=[SMEM] * 3 + [ANY, VMEM],
        out_specs=VMEM,
        scratch_shapes=[pltpu.VMEM((blocks, tiles, rows, depth), everything.dtype), pltpu.SemaphoreType.DMA((1,))],
        compiler_params=pltpu.CompilerParams(vmem_limit_bytes=VMEM_BYTES),
    )(lists, live, jnp.zeros((1,), jnp.int32), everything, integrals)


def cut_kernel(whole, amplitudes, lists, counts, head, tail, amplitudes_out, table, lists_v, counts_s, sems):
    tile_dev, slots = lists_v.shape
    ready = head.shape[0] // slots
    small = [pltpu.make_async_copy(lists, lists_v, sems.at[0]), pltpu.make_async_copy(counts, counts_s, sems.at[1])]
    targets = [head.at[pl.ds(n * slots, slots)] for n in range(ready)]
    targets += [tail.at[pl.ds(n * slots, slots)] for n in range(tile_dev - ready)]
    large = [pltpu.make_async_copy(whole.at[a], target, sems.at[2 + a]) for a, target in enumerate(targets)]
    large.append(pltpu.make_async_copy(amplitudes, amplitudes_out, sems.at[2 + tile_dev]))
    for copy in small + large:
        copy.start()
    head[ready * slots] = jnp.zeros(head.shape[1:], head.dtype)
    for copy in small:
        copy.wait()
    lane = lax.broadcasted_iota(jnp.int32, table.shape, 1)
    values = jnp.zeros(table.shape, jnp.int32)
    for a in range(tile_dev):
        values = jnp.where(lane == a, counts_s[a], values)
    table[...] = values
    table[:tile_dev, :slots] = lists_v[...]
    head[ready * slots, :TABLE_ROWS] = table[...].astype(jnp.float32).astype(head.dtype)
    for copy in large:
        copy.wait()


def cut(whole, amplitudes, lists, counts, ready):
    tile_dev, slots = lists.shape
    sizes = (ready * slots + 1, (tile_dev - ready) * slots)
    placed = [pltpu.with_memory_space_constraint(x, pltpu.HBM) for x in (whole, amplitudes, lists, counts)]
    return pl.pallas_call(
        cut_kernel,
        out_shape=tuple(jax.ShapeDtypeStruct((n,) + whole.shape[2:], whole.dtype) for n in sizes)
        + (
            jax.ShapeDtypeStruct(amplitudes.shape, amplitudes.dtype),
            jax.ShapeDtypeStruct((TABLE_ROWS, whole.shape[3]), jnp.int32),
        ),
        in_specs=[HBM] * 4,
        out_specs=(VMEM,) * 4,
        scratch_shapes=[
            pltpu.VMEM(lists.shape, lists.dtype),
            pltpu.SMEM(counts.shape, counts.dtype),
            pltpu.SemaphoreType.DMA((3 + tile_dev,)),
        ],
        compiler_params=pltpu.CompilerParams(vmem_limit_bytes=VMEM_BYTES),
    )(*placed)


def live_slots(table_ref, a, group, slots):
    return jnp.clip(table_ref[TABLE_ROWS - 1, a] - group * slots, 0, slots)


def own_kernel(layout, slots, place_ref, table_v, *refs):
    count = len(layout)
    pieces, (head, tail, sums_ref, stage, table, sem) = refs[:count], refs[count:]
    ready = head.shape[0] // slots
    blocks, _, rows, _ = stage.shape
    tile_dev, _, width = sums_ref.shape
    copy = pltpu.make_async_copy(table_v, table, sem)
    copy.start()
    for piece, (mask, first) in zip(pieces, layout):
        tiles = piece.shape[0]
        stage[first, pl.ds((place_ref[0] ^ mask) * tiles, tiles)] = piece[...]
    copy.wait()
    for a in range(tile_dev):
        part, base = (head, a * slots) if a < ready else (tail, (a - ready) * slots)
        total = jnp.zeros((blocks * rows, width), jnp.float32)
        live = live_slots(table, a, place_ref[1], slots)
        blocks_of = lambda s, part=part, base=base: part[base + s]
        sums_ref[a] = contract(total, table, a, live, slots, stage, blocks_of)


def add_other(tiles, slots, table, place_ref, stage, sums_ref, others, own_ref, far_ref):
    rows, width = own_ref.shape[0], sums_ref.shape[2]
    for n, a in enumerate(tiles):
        live = live_slots(table, a, place_ref[1] ^ 1, slots)
        blocks_of = lambda s, n=n: others[n * slots + s]
        total = contract(sums_ref[a], table, a, live, slots, stage, blocks_of)
        own_ref[:, n * width:(n + 1) * width] = total[:rows]
        far_ref[:, n * width:(n + 1) * width] = total[rows:]


def head_kernel(tiles, slots, place_ref, stage, sums_ref, others, own_ref, far_ref, table_v, table, sem):
    table_v[...] = others[len(tiles) * slots, :TABLE_ROWS].astype(jnp.float32).astype(jnp.int32)
    copy = pltpu.make_async_copy(table_v, table, sem)
    copy.start()
    copy.wait()
    add_other(tiles, slots, table, place_ref, stage, sums_ref, others, own_ref, far_ref)


def tail_kernel(tiles, slots, place_ref, table_v, stage, sums_ref, others, own_ref, far_ref, table, sem):
    copy = pltpu.make_async_copy(table_v, table, sem)
    copy.start()
    copy.wait()
    add_other(tiles, slots, table, place_ref, stage, sums_ref, others, own_ref, far_ref)


def on_pairs(amplitudes, tile_counts, tile_lists, integrals, n_vv, n_oo):
    tile_dev, slots, width, depth = integrals.shape
    rows = amplitudes.shape[1]
    tiles = n_vv * tile_dev
    ready = tile_dev - 1
    place = jnp.stack([lax.axis_index("vv"), lax.axis_index("oo")]).astype(jnp.int32)

    far = shift(amplitudes, "oo", n_oo, 2)
    head, tail, amplitudes, table = cut(integrals, amplitudes, tile_lists, tile_counts, ready)
    head_other, tail_other = shift(head, "oo", n_oo, 1), shift(tail, "oo", n_oo, 1)
    far, amplitudes = lax.optimization_barrier((far, amplitudes))
    pieces, layout = [], []
    for first, block in enumerate((amplitudes, far)):
        for mask in (0, 2, 4, 6):
            piece = shift(block, "vv", n_vv, mask) if mask else block
            pieces += [piece, shift(piece, "vv", n_vv, 1)]
            layout += [(mask, first), (mask ^ 1, first)]
    params = pltpu.CompilerParams(vmem_limit_bytes=VMEM_BYTES)
    table_type = jax.ShapeDtypeStruct(table.shape, table.dtype)
    scratch = [pltpu.SMEM(table.shape, table.dtype), pltpu.SemaphoreType.DMA]
    sums, stage = pl.pallas_call(
        lambda *refs: own_kernel(layout, slots, *refs),
        out_shape=(
            jax.ShapeDtypeStruct((tile_dev, 2 * rows, width), jnp.float32),
            jax.ShapeDtypeStruct((2, tiles, rows, depth), amplitudes.dtype),
        ),
        in_specs=[SMEM] + [VMEM] * (len(pieces) + 3),
        out_specs=(VMEM,) * 2,
        scratch_shapes=scratch,
        compiler_params=params,
        cost_estimate=pl.CostEstimate(flops=OWN_FLOPS, bytes_accessed=2**22, transcendentals=0),
    )(place, table, *pieces, head, tail)

    def part(count):
        return jax.ShapeDtypeStruct((rows, count * width), jnp.float32)

    own_head, far_head, table = pl.pallas_call(
        lambda *refs: head_kernel(range(ready), slots, *refs),
        out_shape=(part(ready), part(ready), table_type),
        in_specs=[SMEM] + [VMEM] * 3,
        out_specs=(VMEM,) * 3,
        scratch_shapes=scratch,
        compiler_params=params,
        cost_estimate=pl.CostEstimate(flops=HEAD_FLOPS, bytes_accessed=2**21, transcendentals=0),
    )(place, stage, sums, head_other)
    own_tail, far_tail = pl.pallas_call(
        lambda *refs: tail_kernel(range(ready, tile_dev), slots, *refs),
        out_shape=(part(tile_dev - ready),) * 2,
        in_specs=[SMEM] + [VMEM] * 4,
        out_specs=(VMEM,) * 2,
        scratch_shapes=scratch,
        compiler_params=params,
        cost_estimate=pl.CostEstimate(flops=2**28, bytes_accessed=2**21, transcendentals=0),
    )(place, table, stage, sums, tail_other)
    left = own_head + shift(far_head, "oo", n_oo, 2)
    right = own_tail + shift(far_tail, "oo", n_oo, 2)
    return jnp.concatenate([left, right], axis=1)


def on_device(amplitudes, tile_counts, tile_lists, integrals, n_vv, n_oo):
    if (n_vv, n_oo) == (8, 4):
        return on_pairs(amplitudes, tile_counts, tile_lists, integrals, n_vv, n_oo)
    slots = tile_lists.shape[1]
    live = jnp.clip(tile_counts - lax.axis_index("oo") * slots, 0, slots)
    rows = lax.all_gather(amplitudes, "oo", axis=0, tiled=False)
    everything = lax.all_gather(rows, "vv", axis=1, tiled=True)
    parts = plain_partials(tile_lists, live, everything, integrals)
    return lax.psum_scatter(parts.reshape(-1, parts.shape[2]), "oo", scatter_dimension=0, tiled=True)


def solution(mesh):
    n_vv, n_oo = mesh.shape["vv"], mesh.shape["oo"]
    placed = (P("vv", "oo", None), P("vv"), P("vv", "oo"), P("vv", "oo", None, None))
    return jax.shard_map(
        lambda *args: on_device(*args, n_vv, n_oo),
        mesh=mesh, in_specs=placed, out_specs=P("oo", "vv"), check_vma=False,
    )
```

```python
import jax
import jax.numpy as jnp
from jax import lax
from jax.experimental import pallas as pl
from jax.experimental.pallas import tpu as pltpu
from jax.sharding import PartitionSpec as P

VMEM_BYTES = 48 * 1024 * 1024
UNROLL = 4
OWN_FLOPS = 3750000000
HEAD_FLOPS = 250000000
TABLE_ROWS = 16
PARTS = 2
SMEM = pl.BlockSpec(memory_space=pltpu.SMEM)
VMEM = pl.BlockSpec(memory_space=pltpu.VMEM)
ANY = pl.BlockSpec(memory_space=pl.ANY)
HBM = pl.BlockSpec(memory_space=pltpu.HBM)


def shift(value, axis, size, mask):
    return lax.ppermute(value, axis, [(j, j ^ mask) for j in range(size)])


def contract(total, lists_ref, a, live, slots, stage, blocks_of, flip=False):
    blocks, _, rows, depth = stage.shape
    dims = (((1,), (1,)), ((), ()))

    def pair(s):
        sides, weights = [], []
        for slot in (s, s + 1):
            safe = jnp.minimum(slot, slots - 1)
            block = blocks_of(safe)
            sides.append(stage[:, lists_ref[a, safe]].reshape(blocks * rows, depth))
            weights.append(jnp.where(slot < live, block, jnp.zeros_like(block)))
        sides, weights = jnp.concatenate(sides, axis=1), jnp.concatenate(weights, axis=1)
        left, right = (weights, sides) if flip else (sides, weights)
        return lax.dot_general(left, right, dims, preferred_element_type=jnp.float32)

    def step(group, total):
        for offset in range(0, UNROLL, 2):
            total = total + pair(UNROLL * group + offset)
        return total

    return lax.fori_loop(0, (live + UNROLL - 1) // UNROLL, step, total)


def plain_kernel(lists_ref, live_ref, place_ref, piece, integrals_ref, out_ref, stage, sems):
    copy = pltpu.make_async_copy(piece, stage, sems.at[0])
    copy.start()
    copy.wait()
    tile_dev, _, width, _ = integrals_ref.shape
    blocks, _, rows, _ = stage.shape
    for a in range(tile_dev):
        zero = jnp.zeros((blocks * rows, width), jnp.float32)
        total = contract(zero, lists_ref, a, live_ref[a], lists_ref.shape[1], stage, lambda s, a=a: integrals_ref[a, s])
        for k in range(blocks):
            out_ref[k, :, a * width:(a + 1) * width] = total[k * rows:(k + 1) * rows]


def plain_partials(lists, live, everything, integrals):
    blocks, tiles, rows, depth = everything.shape
    tile_dev, _, width, _ = integrals.shape
    return pl.pallas_call(
        plain_kernel,
        out_shape=jax.ShapeDtypeStruct((blocks, rows, tile_dev * width), jnp.float32),
        in_specs=[SMEM] * 3 + [ANY, VMEM],
        out_specs=VMEM,
        scratch_shapes=[pltpu.VMEM((blocks, tiles, rows, depth), everything.dtype), pltpu.SemaphoreType.DMA((1,))],
        compiler_params=pltpu.CompilerParams(vmem_limit_bytes=VMEM_BYTES),
    )(lists, live, jnp.zeros((1,), jnp.int32), everything, integrals)


def split(tile_dev, slots, width):
    size = width // PARTS
    places = [[(0, a * slots * width, width)] for a in range(tile_dev - 1)]
    places.append([(1 + n, 0, size) for n in range(PARTS)])
    return places, [(tile_dev - 1) * slots * width] + [slots * size] * PARTS


def cut_kernel(whole, amplitudes, lists, counts, *refs):
    arrays, (amplitudes_out, table, lists_v, counts_s, sems) = refs[:1 + PARTS], refs[1 + PARTS:]
    head = arrays[0]
    tile_dev, slots, width, _ = whole.shape
    places, sizes = split(tile_dev, slots, width)
    small = [(lists, lists_v), (counts, counts_s)]
    large = [(amplitudes, amplitudes_out)]
    for a, parts in enumerate(places):
        done = 0
        for array, first, size in parts:
            target = arrays[array]
            if size == width:
                large.append((whole.at[a], target.at[pl.ds(first, slots * size)].reshape(slots, size, whole.shape[3])))
                continue
            for s in range(slots):
                large.append((whole.at[a, s, pl.ds(done, size)], target.at[pl.ds(first + s * size, size)]))
            done += size
    copies = [pltpu.make_async_copy(x, y, sems.at[n]) for n, (x, y) in enumerate(small + large)]
    for copy in copies:
        copy.start()
    for copy in copies[:2]:
        copy.wait()
    lane = lax.broadcasted_iota(jnp.int32, table.shape, 1)
    values = jnp.zeros(table.shape, jnp.int32)
    for a in range(tile_dev):
        values = jnp.where(lane == a, counts_s[a], values)
    table[...] = values
    table[:tile_dev, :slots] = lists_v[...]
    head[sizes[0]:] = table[...].astype(jnp.float32).astype(head.dtype)
    for copy in copies[2:]:
        copy.wait()


def cut(whole, amplitudes, lists, counts):
    tile_dev, slots, width, depth = whole.shape
    sizes = split(tile_dev, slots, width)[1]
    placed = [pltpu.with_memory_space_constraint(x, pltpu.HBM) for x in (whole, amplitudes, lists, counts)]
    return pl.pallas_call(
        cut_kernel,
        out_shape=(
            jax.ShapeDtypeStruct((sizes[0] + TABLE_ROWS, depth), whole.dtype),
            *(jax.ShapeDtypeStruct((size, depth), whole.dtype) for size in sizes[1:]),
            jax.ShapeDtypeStruct(amplitudes.shape, amplitudes.dtype),
            jax.ShapeDtypeStruct((TABLE_ROWS, depth), jnp.int32),
        ),
        in_specs=[HBM] * 4,
        out_specs=(VMEM,) * (3 + PARTS),
        scratch_shapes=[
            pltpu.VMEM(lists.shape, lists.dtype),
            pltpu.SMEM(counts.shape, counts.dtype),
            pltpu.SemaphoreType.DMA((3 + (tile_dev - 1) + PARTS * slots,)),
        ],
        compiler_params=pltpu.CompilerParams(vmem_limit_bytes=VMEM_BYTES),
    )(*placed)


def stack_kernel(first, second, out):
    out[0] = first[...]
    out[1] = second[...]


def live_slots(table_ref, a, group, slots):
    return jnp.clip(table_ref[TABLE_ROWS - 1, a] - group * slots, 0, slots)


def blocks_at(arrays, parts):
    def block(s):
        rows = [arrays[array][pl.ds(pl.multiple_of(first + s * size, 16), size)] for array, first, size in parts]
        return rows[0] if len(rows) == 1 else jnp.concatenate(rows, axis=0)

    return block


def own_kernel(masks, slots, place_ref, table_v, *refs):
    count = len(masks)
    pieces, arrays, (sums_ref, last_ref, stage, table, sem) = refs[:count], refs[count:-5], refs[-5:]
    blocks, _, rows, _ = stage.shape
    before, _, width = sums_ref.shape
    copy = pltpu.make_async_copy(table_v, table, sem)
    copy.start()
    for piece, mask in zip(pieces, masks):
        tiles = piece.shape[1]
        stage[:, pl.ds((place_ref[0] ^ mask) * tiles, tiles)] = piece[...]
    copy.wait()
    places = split(before + 1, slots, width)[0]
    for a, parts in enumerate(places):
        flip = a == before
        total = jnp.zeros((width, blocks * rows) if flip else (blocks * rows, width), jnp.float32)
        live = live_slots(table, a, place_ref[1], slots)
        total = contract(total, table, a, live, slots, stage, blocks_at(arrays, parts), flip)
        if flip:
            last_ref[...] = total
        else:
            sums_ref[a] = total


def head_kernel(slots, place_ref, stage, sums_ref, others, own_ref, far_ref, table_v, table, sem):
    before, both, width = sums_ref.shape
    rows = both // 2
    places, sizes = split(before + 1, slots, width)
    table_v[...] = others[sizes[0]:].astype(jnp.float32).astype(jnp.int32)
    copy = pltpu.make_async_copy(table_v, table, sem)
    copy.start()
    copy.wait()
    for a in range(before):
        live = live_slots(table, a, place_ref[1] ^ 1, slots)
        total = contract(sums_ref[a], table, a, live, slots, stage, blocks_at((others,), places[a]))
        own_ref[a * rows:(a + 1) * rows] = total[:rows]
        far_ref[a * rows:(a + 1) * rows] = total[rows:]


def pick_kernel(a, slots, place_ref, table_v, stage, picked, table, sem):
    blocks, _, rows, depth = stage.shape
    copy = pltpu.make_async_copy(table_v, table, sem)
    copy.start()
    copy.wait()
    live = live_slots(table, a, place_ref[1] ^ 1, slots)
    for s in range(slots):
        block = stage[:, table[a, s]].reshape(blocks * rows, depth)
        picked[:, s * depth:(s + 1) * depth] = jnp.where(s < live, block, jnp.zeros_like(block))


def tail_kernel(slots, n, last_ref, picked, others, own_ref, far_ref):
    size, rows = own_ref.shape
    depth = others.shape[1]
    total = last_ref[n * size:(n + 1) * size]
    for s in range(0, slots, 2):
        some = range(s, min(s + 2, slots))
        weights = jnp.concatenate([others[m * size:(m + 1) * size] for m in some], axis=1)
        sides = picked[:, s * depth:(s + len(some)) * depth]
        total = total + lax.dot_general(weights, sides, (((1,), (1,)), ((), ())), preferred_element_type=jnp.float32)
    own_ref[...] = total[:, :rows]
    far_ref[...] = total[:, rows:]


def join_kernel(*refs):
    own, got, out = refs[:1 + PARTS], refs[1 + PARTS:-1], refs[-1]
    rows = out.shape[0]
    before = own[0].shape[0] // rows
    width = out.shape[1] // (before + 1)
    for a in range(before):
        part = pl.ds(a * rows, rows)
        out[:, a * width:(a + 1) * width] = own[0][part] + got[0][part]
    last = jnp.concatenate([own[n][...] + got[n][...] for n in range(1, 1 + PARTS)], axis=0)
    out[:, before * width:] = jnp.transpose(last)


def on_pairs(amplitudes, tile_counts, tile_lists, integrals, n_vv, n_oo):
    tile_dev, slots, width, depth = integrals.shape
    rows = amplitudes.shape[1]
    tiles = n_vv * tile_dev
    before = tile_dev - 1
    place = jnp.stack([lax.axis_index("vv"), lax.axis_index("oo")]).astype(jnp.int32)

    far = shift(amplitudes, "oo", n_oo, 2)
    *arrays, amplitudes, table = cut(integrals, amplitudes, tile_lists, tile_counts)
    others = [shift(array, "oo", n_oo, 1) for array in arrays]
    block = pl.pallas_call(
        stack_kernel,
        out_shape=jax.ShapeDtypeStruct((2,) + amplitudes.shape, amplitudes.dtype),
        in_specs=[VMEM] * 2,
        out_specs=VMEM,
        compiler_params=pltpu.CompilerParams(vmem_limit_bytes=VMEM_BYTES),
        cost_estimate=pl.CostEstimate(flops=2**20, bytes_accessed=2**19, transcendentals=0),
    )(amplitudes, far)
    pieces, masks = [], []
    for mask in (0, 2, 4, 6):
        piece = shift(block, "vv", n_vv, mask) if mask else block
        pieces += [piece, shift(piece, "vv", n_vv, 1)]
        masks += [mask, mask ^ 1]
    scratch = [pltpu.SMEM(table.shape, table.dtype), pltpu.SemaphoreType.DMA]

    def call(kernel, out, n_smem, n_vmem, scratch, flops):
        return pl.pallas_call(
            kernel,
            out_shape=out,
            in_specs=[SMEM] * n_smem + [VMEM] * n_vmem,
            out_specs=jax.tree.map(lambda _: VMEM, out),
            scratch_shapes=scratch,
            compiler_params=pltpu.CompilerParams(vmem_limit_bytes=VMEM_BYTES),
            cost_estimate=pl.CostEstimate(flops=flops, bytes_accessed=2**21, transcendentals=0),
        )

    def f32(*shape):
        return jax.ShapeDtypeStruct(shape, jnp.float32)

    sums, last, stage = call(
        lambda *refs: own_kernel(masks, slots, *refs),
        (f32(before, 2 * rows, width), f32(width, 2 * rows), jax.ShapeDtypeStruct((2, tiles, rows, depth), far.dtype)),
        1, len(pieces) + 2 + PARTS, scratch, OWN_FLOPS,
    )(place, table, *pieces, *arrays)
    part = f32(before * rows, width)
    own, away, table = call(
        lambda *refs: head_kernel(slots, *refs),
        (part, part, jax.ShapeDtypeStruct(table.shape, table.dtype)),
        1, 3, scratch, HEAD_FLOPS,
    )(place, stage, sums, others[0])
    picked = call(
        lambda *refs: pick_kernel(before, slots, *refs),
        jax.ShapeDtypeStruct((2 * rows, slots * depth), far.dtype),
        1, 2, scratch, 2**28,
    )(place, table, stage)
    owns, gots = [own], [shift(away, "oo", n_oo, 2)]
    for n in range(PARTS):
        own, away = call(
            lambda *refs, n=n: tail_kernel(slots, n, *refs), (f32(width // PARTS, rows),) * 2, 0, 3, [], 2**28
        )(last, picked, others[1 + n])
        owns.append(own)
        gots.append(shift(away, "oo", n_oo, 2))
    return call(join_kernel, f32(rows, tile_dev * width), 0, 2 * (1 + PARTS), [], 2**20)(*owns, *gots)


def on_device(amplitudes, tile_counts, tile_lists, integrals, n_vv, n_oo):
    if (n_vv, n_oo) == (8, 4):
        return on_pairs(amplitudes, tile_counts, tile_lists, integrals, n_vv, n_oo)
    slots = tile_lists.shape[1]
    live = jnp.clip(tile_counts - lax.axis_index("oo") * slots, 0, slots)
    rows = lax.all_gather(amplitudes, "oo", axis=0, tiled=False)
    everything = lax.all_gather(rows, "vv", axis=1, tiled=True)
    parts = plain_partials(tile_lists, live, everything, integrals)
    return lax.psum_scatter(parts.reshape(-1, parts.shape[2]), "oo", scatter_dimension=0, tiled=True)


def solution(mesh):
    n_vv, n_oo = mesh.shape["vv"], mesh.shape["oo"]
    placed = (P("vv", "oo", None), P("vv"), P("vv", "oo"), P("vv", "oo", None, None))
    return jax.shard_map(
        lambda *args: on_device(*args, n_vv, n_oo),
        mesh=mesh, in_specs=placed, out_specs=P("oo", "vv"), check_vma=False,
    )
```

```python
import jax
import jax.numpy as jnp
from jax import lax
from jax.experimental import pallas as pl
from jax.experimental.pallas import tpu as pltpu
from jax.sharding import PartitionSpec as P

VMEM_BYTES = 48 * 1024 * 1024
UNROLL = 4
OWN_FLOPS = 3750000000
HEAD_FLOPS = 250000000
TABLE_ROWS = 16
PARTS = 2
SMEM = pl.BlockSpec(memory_space=pltpu.SMEM)
VMEM = pl.BlockSpec(memory_space=pltpu.VMEM)
ANY = pl.BlockSpec(memory_space=pl.ANY)
HBM = pl.BlockSpec(memory_space=pltpu.HBM)


def shift(value, axis, size, mask):
    return lax.ppermute(value, axis, [(j, j ^ mask) for j in range(size)])


def contract(total, lists_ref, a, live, slots, stage, blocks_of, flip=False):
    blocks, _, rows, depth = stage.shape
    dims = (((1,), (1,)), ((), ()))

    def pair(s):
        sides, weights = [], []
        for slot in (s, s + 1):
            safe = jnp.minimum(slot, slots - 1)
            block = blocks_of(safe)
            sides.append(stage[:, lists_ref[a, safe]].reshape(blocks * rows, depth))
            weights.append(jnp.where(slot < live, block, jnp.zeros_like(block)))
        sides, weights = jnp.concatenate(sides, axis=1), jnp.concatenate(weights, axis=1)
        left, right = (weights, sides) if flip else (sides, weights)
        return lax.dot_general(left, right, dims, preferred_element_type=jnp.float32)

    def step(group, total):
        for offset in range(0, UNROLL, 2):
            total = total + pair(UNROLL * group + offset)
        return total

    return lax.fori_loop(0, (live + UNROLL - 1) // UNROLL, step, total)


def plain_kernel(lists_ref, live_ref, place_ref, piece, integrals_ref, out_ref, stage, sems):
    copy = pltpu.make_async_copy(piece, stage, sems.at[0])
    copy.start()
    copy.wait()
    tile_dev, _, width, _ = integrals_ref.shape
    blocks, _, rows, _ = stage.shape
    for a in range(tile_dev):
        zero = jnp.zeros((blocks * rows, width), jnp.float32)
        total = contract(zero, lists_ref, a, live_ref[a], lists_ref.shape[1], stage, lambda s, a=a: integrals_ref[a, s])
        for k in range(blocks):
            out_ref[k, :, a * width:(a + 1) * width] = total[k * rows:(k + 1) * rows]


def plain_partials(lists, live, everything, integrals):
    blocks, tiles, rows, depth = everything.shape
    tile_dev, _, width, _ = integrals.shape
    return pl.pallas_call(
        plain_kernel,
        out_shape=jax.ShapeDtypeStruct((blocks, rows, tile_dev * width), jnp.float32),
        in_specs=[SMEM] * 3 + [ANY, VMEM],
        out_specs=VMEM,
        scratch_shapes=[pltpu.VMEM((blocks, tiles, rows, depth), everything.dtype), pltpu.SemaphoreType.DMA((1,))],
        compiler_params=pltpu.CompilerParams(vmem_limit_bytes=VMEM_BYTES),
    )(lists, live, jnp.zeros((1,), jnp.int32), everything, integrals)


def split(tile_dev, slots, width):
    size = width // PARTS
    places = [[(0, a * slots * width, width)] for a in range(tile_dev - 1)]
    places.append([(1 + n, 0, size) for n in range(PARTS)])
    return places, [(tile_dev - 1) * slots * width] + [slots * size] * PARTS


def head_cut_kernel(whole, lists, counts, head, table, lists_v, counts_s, sems):
    tile_dev, slots, width, depth = whole.shape
    pairs = [(lists, lists_v), (counts, counts_s)]
    for a in range(tile_dev - 1):
        rows = slots * width
        pairs.append((whole.at[a], head.at[pl.ds(a * rows, rows)].reshape(slots, width, depth)))
    copies = [pltpu.make_async_copy(x, y, sems.at[n]) for n, (x, y) in enumerate(pairs)]
    for copy in copies:
        copy.start()
    for copy in copies[:2]:
        copy.wait()
    lane = lax.broadcasted_iota(jnp.int32, table.shape, 1)
    values = jnp.zeros(table.shape, jnp.int32)
    for a in range(tile_dev):
        values = jnp.where(lane == a, counts_s[a], values)
    table[...] = values
    table[:tile_dev, :slots] = lists_v[...]
    head[(tile_dev - 1) * slots * width:] = table[...].astype(jnp.float32).astype(head.dtype)
    for copy in copies[2:]:
        copy.wait()


def rest_cut_kernel(whole, amplitudes, *refs):
    parts, (amplitudes_out, sems) = refs[:PARTS], refs[PARTS:]
    tile_dev, slots, width, _ = whole.shape
    size = width // PARTS
    pairs = [(amplitudes, amplitudes_out)]
    for n, part in enumerate(parts):
        for s in range(slots):
            pairs.append((whole.at[tile_dev - 1, s, pl.ds(n * size, size)], part.at[pl.ds(s * size, size)]))
    copies = [pltpu.make_async_copy(x, y, sems.at[n]) for n, (x, y) in enumerate(pairs)]
    for copy in copies:
        copy.start()
    for copy in copies:
        copy.wait()


def cut(whole, amplitudes, lists, counts):
    tile_dev, slots, width, depth = whole.shape
    sizes = split(tile_dev, slots, width)[1]
    whole, amplitudes, lists, counts = (
        pltpu.with_memory_space_constraint(x, pltpu.HBM) for x in (whole, amplitudes, lists, counts)
    )
    params = pltpu.CompilerParams(vmem_limit_bytes=VMEM_BYTES)
    head, table = pl.pallas_call(
        head_cut_kernel,
        out_shape=(
            jax.ShapeDtypeStruct((sizes[0] + TABLE_ROWS, depth), whole.dtype),
            jax.ShapeDtypeStruct((TABLE_ROWS, depth), jnp.int32),
        ),
        in_specs=[HBM] * 3,
        out_specs=(VMEM,) * 2,
        scratch_shapes=[
            pltpu.VMEM(lists.shape, lists.dtype),
            pltpu.SMEM(counts.shape, counts.dtype),
            pltpu.SemaphoreType.DMA((1 + tile_dev,)),
        ],
        compiler_params=params,
    )(whole, lists, counts)
    *parts, amplitudes = pl.pallas_call(
        rest_cut_kernel,
        out_shape=(jax.ShapeDtypeStruct((sizes[1], depth), whole.dtype),) * PARTS
        + (jax.ShapeDtypeStruct(amplitudes.shape, amplitudes.dtype),),
        in_specs=[HBM] * 2,
        out_specs=(VMEM,) * (1 + PARTS),
        scratch_shapes=[pltpu.SemaphoreType.DMA((1 + PARTS * slots,))],
        compiler_params=params,
        cost_estimate=pl.CostEstimate(flops=2**20, bytes_accessed=2**19, transcendentals=0),
    )(whole, amplitudes)
    return [head, *parts, amplitudes, table]


def stack_kernel(first, second, out):
    out[0] = first[...]
    out[1] = second[...]


def live_slots(table_ref, a, group, slots):
    return jnp.clip(table_ref[TABLE_ROWS - 1, a] - group * slots, 0, slots)


def blocks_at(arrays, parts):
    def block(s):
        rows = [arrays[array][pl.ds(pl.multiple_of(first + s * size, 16), size)] for array, first, size in parts]
        return rows[0] if len(rows) == 1 else jnp.concatenate(rows, axis=0)

    return block


def own_kernel(masks, slots, place_ref, table_v, *refs):
    count = len(masks)
    pieces, arrays, (sums_ref, last_ref, stage, table, sem) = refs[:count], refs[count:-5], refs[-5:]
    blocks, _, rows, _ = stage.shape
    before, _, width = sums_ref.shape
    copy = pltpu.make_async_copy(table_v, table, sem)
    copy.start()
    for piece, mask in zip(pieces, masks):
        tiles = piece.shape[1]
        stage[:, pl.ds((place_ref[0] ^ mask) * tiles, tiles)] = piece[...]
    copy.wait()
    places = split(before + 1, slots, width)[0]
    for a, parts in enumerate(places):
        flip = a == before
        total = jnp.zeros((width, blocks * rows) if flip else (blocks * rows, width), jnp.float32)
        live = live_slots(table, a, place_ref[1], slots)
        total = contract(total, table, a, live, slots, stage, blocks_at(arrays, parts), flip)
        if flip:
            last_ref[...] = total
        else:
            sums_ref[a] = total


def head_kernel(slots, place_ref, stage, sums_ref, others, own_ref, far_ref, table_v, table, sem):
    before, both, width = sums_ref.shape
    rows = both // 2
    places, sizes = split(before + 1, slots, width)
    table_v[...] = others[sizes[0]:].astype(jnp.float32).astype(jnp.int32)
    copy = pltpu.make_async_copy(table_v, table, sem)
    copy.start()
    copy.wait()
    for a in range(before):
        live = live_slots(table, a, place_ref[1] ^ 1, slots)
        total = contract(sums_ref[a], table, a, live, slots, stage, blocks_at((others,), places[a]))
        own_ref[a * rows:(a + 1) * rows] = total[:rows]
        far_ref[a * rows:(a + 1) * rows] = total[rows:]


def pick_kernel(a, slots, place_ref, table_v, stage, picked, table, sem):
    blocks, _, rows, depth = stage.shape
    copy = pltpu.make_async_copy(table_v, table, sem)
    copy.start()
    copy.wait()
    live = live_slots(table, a, place_ref[1] ^ 1, slots)
    for s in range(slots):
        block = stage[:, table[a, s]].reshape(blocks * rows, depth)
        picked[:, s * depth:(s + 1) * depth] = jnp.where(s < live, block, jnp.zeros_like(block))


def tail_kernel(slots, n, last_ref, picked, others, own_ref, far_ref):
    size, rows = own_ref.shape
    depth = others.shape[1]
    total = last_ref[n * size:(n + 1) * size]
    for s in range(0, slots, 2):
        some = range(s, min(s + 2, slots))
        weights = jnp.concatenate([others[m * size:(m + 1) * size] for m in some], axis=1)
        sides = picked[:, s * depth:(s + len(some)) * depth]
        total = total + lax.dot_general(weights, sides, (((1,), (1,)), ((), ())), preferred_element_type=jnp.float32)
    own_ref[...] = total[:, :rows]
    far_ref[...] = total[:, rows:]


def join_kernel(*refs):
    own, got, out = refs[:1 + PARTS], refs[1 + PARTS:-1], refs[-1]
    rows = out.shape[0]
    before = own[0].shape[0] // rows
    width = out.shape[1] // (before + 1)
    for a in range(before):
        part = pl.ds(a * rows, rows)
        out[:, a * width:(a + 1) * width] = own[0][part] + got[0][part]
    last = jnp.concatenate([own[n][...] + got[n][...] for n in range(1, 1 + PARTS)], axis=0)
    out[:, before * width:] = jnp.transpose(last)


def on_pairs(amplitudes, tile_counts, tile_lists, integrals, n_vv, n_oo):
    tile_dev, slots, width, depth = integrals.shape
    rows = amplitudes.shape[1]
    tiles = n_vv * tile_dev
    before = tile_dev - 1
    place = jnp.stack([lax.axis_index("vv"), lax.axis_index("oo")]).astype(jnp.int32)

    far = shift(amplitudes, "oo", n_oo, 2)
    *arrays, amplitudes, table = cut(integrals, amplitudes, tile_lists, tile_counts)
    others = [shift(array, "oo", n_oo, 1) for array in arrays]
    block = pl.pallas_call(
        stack_kernel,
        out_shape=jax.ShapeDtypeStruct((2,) + amplitudes.shape, amplitudes.dtype),
        in_specs=[VMEM] * 2,
        out_specs=VMEM,
        compiler_params=pltpu.CompilerParams(vmem_limit_bytes=VMEM_BYTES),
        cost_estimate=pl.CostEstimate(flops=2**20, bytes_accessed=2**19, transcendentals=0),
    )(amplitudes, far)
    pieces, masks = [], []
    for mask in (0, 2, 4, 6):
        piece = shift(block, "vv", n_vv, mask) if mask else block
        pieces += [piece, shift(piece, "vv", n_vv, 1)]
        masks += [mask, mask ^ 1]
    scratch = [pltpu.SMEM(table.shape, table.dtype), pltpu.SemaphoreType.DMA]

    def call(kernel, out, n_smem, n_vmem, scratch, flops):
        return pl.pallas_call(
            kernel,
            out_shape=out,
            in_specs=[SMEM] * n_smem + [VMEM] * n_vmem,
            out_specs=jax.tree.map(lambda _: VMEM, out),
            scratch_shapes=scratch,
            compiler_params=pltpu.CompilerParams(vmem_limit_bytes=VMEM_BYTES),
            cost_estimate=pl.CostEstimate(flops=flops, bytes_accessed=2**21, transcendentals=0),
        )

    def f32(*shape):
        return jax.ShapeDtypeStruct(shape, jnp.float32)

    sums, last, stage = call(
        lambda *refs: own_kernel(masks, slots, *refs),
        (f32(before, 2 * rows, width), f32(width, 2 * rows), jax.ShapeDtypeStruct((2, tiles, rows, depth), far.dtype)),
        1, len(pieces) + 2 + PARTS, scratch, OWN_FLOPS,
    )(place, table, *pieces, *arrays)
    part = f32(before * rows, width)
    own, away, table = call(
        lambda *refs: head_kernel(slots, *refs),
        (part, part, jax.ShapeDtypeStruct(table.shape, table.dtype)),
        1, 3, scratch, HEAD_FLOPS,
    )(place, stage, sums, others[0])
    picked = call(
        lambda *refs: pick_kernel(before, slots, *refs),
        jax.ShapeDtypeStruct((2 * rows, slots * depth), far.dtype),
        1, 2, scratch, 2**28,
    )(place, table, stage)
    owns, gots = [own], [shift(away, "oo", n_oo, 2)]
    for n in range(PARTS):
        own, away = call(
            lambda *refs, n=n: tail_kernel(slots, n, *refs), (f32(width // PARTS, rows),) * 2, 0, 3, [], 2**28
        )(last, picked, others[1 + n])
        owns.append(own)
        gots.append(shift(away, "oo", n_oo, 2))
    return call(join_kernel, f32(rows, tile_dev * width), 0, 2 * (1 + PARTS), [], 2**20)(*owns, *gots)


def on_device(amplitudes, tile_counts, tile_lists, integrals, n_vv, n_oo):
    if (n_vv, n_oo) == (8, 4):
        return on_pairs(amplitudes, tile_counts, tile_lists, integrals, n_vv, n_oo)
    slots = tile_lists.shape[1]
    live = jnp.clip(tile_counts - lax.axis_index("oo") * slots, 0, slots)
    rows = lax.all_gather(amplitudes, "oo", axis=0, tiled=False)
    everything = lax.all_gather(rows, "vv", axis=1, tiled=True)
    parts = plain_partials(tile_lists, live, everything, integrals)
    return lax.psum_scatter(parts.reshape(-1, parts.shape[2]), "oo", scatter_dimension=0, tiled=True)


def solution(mesh):
    n_vv, n_oo = mesh.shape["vv"], mesh.shape["oo"]
    placed = (P("vv", "oo", None), P("vv"), P("vv", "oo"), P("vv", "oo", None, None))
    return jax.shard_map(
        lambda *args: on_device(*args, n_vv, n_oo),
        mesh=mesh, in_specs=placed, out_specs=P("oo", "vv"), check_vma=False,
    )
```

```python
import jax
import jax.numpy as jnp
from jax import lax
from jax.experimental import pallas as pl
from jax.experimental.pallas import tpu as pltpu
from jax.sharding import PartitionSpec as P

VMEM_BYTES = 48 * 1024 * 1024
UNROLL = 4
OWN_FLOPS = 3750000000
HEAD_FLOPS = 250000000
SOON = 4
TABLE_ROWS = 16
PARTS = 2
SMEM = pl.BlockSpec(memory_space=pltpu.SMEM)
VMEM = pl.BlockSpec(memory_space=pltpu.VMEM)
ANY = pl.BlockSpec(memory_space=pl.ANY)
HBM = pl.BlockSpec(memory_space=pltpu.HBM)


def shift(value, axis, size, mask):
    return lax.ppermute(value, axis, [(j, j ^ mask) for j in range(size)])


def contract(total, lists_ref, a, live, slots, stage, blocks_of, flip=False):
    blocks, _, rows, depth = stage.shape
    dims = (((1,), (1,)), ((), ()))

    def pair(s):
        sides, weights = [], []
        for slot in (s, s + 1):
            safe = jnp.minimum(slot, slots - 1)
            block = blocks_of(safe)
            sides.append(stage[:, lists_ref[a, safe]].reshape(blocks * rows, depth))
            weights.append(jnp.where(slot < live, block, jnp.zeros_like(block)))
        sides, weights = jnp.concatenate(sides, axis=1), jnp.concatenate(weights, axis=1)
        left, right = (weights, sides) if flip else (sides, weights)
        return lax.dot_general(left, right, dims, preferred_element_type=jnp.float32)

    def step(group, total):
        for offset in range(0, UNROLL, 2):
            total = total + pair(UNROLL * group + offset)
        return total

    return lax.fori_loop(0, (live + UNROLL - 1) // UNROLL, step, total)


def plain_kernel(lists_ref, live_ref, place_ref, piece, integrals_ref, out_ref, stage, sems):
    copy = pltpu.make_async_copy(piece, stage, sems.at[0])
    copy.start()
    copy.wait()
    tile_dev, _, width, _ = integrals_ref.shape
    blocks, _, rows, _ = stage.shape
    for a in range(tile_dev):
        zero = jnp.zeros((blocks * rows, width), jnp.float32)
        total = contract(zero, lists_ref, a, live_ref[a], lists_ref.shape[1], stage, lambda s, a=a: integrals_ref[a, s])
        for k in range(blocks):
            out_ref[k, :, a * width:(a + 1) * width] = total[k * rows:(k + 1) * rows]


def plain_partials(lists, live, everything, integrals):
    blocks, tiles, rows, depth = everything.shape
    tile_dev, _, width, _ = integrals.shape
    return pl.pallas_call(
        plain_kernel,
        out_shape=jax.ShapeDtypeStruct((blocks, rows, tile_dev * width), jnp.float32),
        in_specs=[SMEM] * 3 + [ANY, VMEM],
        out_specs=VMEM,
        scratch_shapes=[pltpu.VMEM((blocks, tiles, rows, depth), everything.dtype), pltpu.SemaphoreType.DMA((1,))],
        compiler_params=pltpu.CompilerParams(vmem_limit_bytes=VMEM_BYTES),
    )(lists, live, jnp.zeros((1,), jnp.int32), everything, integrals)


def split(tile_dev, slots, width):
    size = width // PARTS
    places = [[(0, a * slots * width, width)] for a in range(tile_dev - 1)]
    places.append([(1 + n, 0, size) for n in range(PARTS)])
    return places, [(tile_dev - 1) * slots * width] + [slots * size] * PARTS


def head_cut_kernel(whole, lists, counts, head, table, lists_v, counts_s, sems):
    tile_dev, slots, width, depth = whole.shape
    pairs = [(lists, lists_v), (counts, counts_s)]
    for a in range(tile_dev - 1):
        rows = slots * width
        pairs.append((whole.at[a], head.at[pl.ds(a * rows, rows)].reshape(slots, width, depth)))
    copies = [pltpu.make_async_copy(x, y, sems.at[n]) for n, (x, y) in enumerate(pairs)]
    for copy in copies:
        copy.start()
    for copy in copies[:2]:
        copy.wait()
    lane = lax.broadcasted_iota(jnp.int32, table.shape, 1)
    values = jnp.zeros(table.shape, jnp.int32)
    for a in range(tile_dev):
        values = jnp.where(lane == a, counts_s[a], values)
    table[...] = values
    table[:tile_dev, :slots] = lists_v[...]
    head[(tile_dev - 1) * slots * width:] = table[...].astype(jnp.float32).astype(head.dtype)
    for copy in copies[2:]:
        copy.wait()


def rest_cut_kernel(whole, amplitudes, *refs):
    parts, (amplitudes_out, sems) = refs[:PARTS], refs[PARTS:]
    tile_dev, slots, width, _ = whole.shape
    size = width // PARTS
    pairs = [(amplitudes, amplitudes_out)]
    for n, part in enumerate(parts):
        for s in range(slots):
            pairs.append((whole.at[tile_dev - 1, s, pl.ds(n * size, size)], part.at[pl.ds(s * size, size)]))
    copies = [pltpu.make_async_copy(x, y, sems.at[n]) for n, (x, y) in enumerate(pairs)]
    for copy in copies:
        copy.start()
    for copy in copies:
        copy.wait()


def cut(whole, amplitudes, lists, counts):
    tile_dev, slots, width, depth = whole.shape
    sizes = split(tile_dev, slots, width)[1]
    whole, amplitudes, lists, counts = (
        pltpu.with_memory_space_constraint(x, pltpu.HBM) for x in (whole, amplitudes, lists, counts)
    )
    params = pltpu.CompilerParams(vmem_limit_bytes=VMEM_BYTES)
    head, table = pl.pallas_call(
        head_cut_kernel,
        out_shape=(
            jax.ShapeDtypeStruct((sizes[0] + TABLE_ROWS, depth), whole.dtype),
            jax.ShapeDtypeStruct((TABLE_ROWS, depth), jnp.int32),
        ),
        in_specs=[HBM] * 3,
        out_specs=(VMEM,) * 2,
        scratch_shapes=[
            pltpu.VMEM(lists.shape, lists.dtype),
            pltpu.SMEM(counts.shape, counts.dtype),
            pltpu.SemaphoreType.DMA((1 + tile_dev,)),
        ],
        compiler_params=params,
    )(whole, lists, counts)
    *parts, amplitudes = pl.pallas_call(
        rest_cut_kernel,
        out_shape=(jax.ShapeDtypeStruct((sizes[1], depth), whole.dtype),) * PARTS
        + (jax.ShapeDtypeStruct(amplitudes.shape, amplitudes.dtype),),
        in_specs=[HBM] * 2,
        out_specs=(VMEM,) * (1 + PARTS),
        scratch_shapes=[pltpu.SemaphoreType.DMA((1 + PARTS * slots,))],
        compiler_params=params,
        cost_estimate=pl.CostEstimate(flops=2**20, bytes_accessed=2**19, transcendentals=0),
    )(whole, amplitudes)
    return [head, *parts, amplitudes, table]


def stack_kernel(first, second, out):
    out[0] = first[...]
    out[1] = second[...]


def live_slots(table_ref, a, group, slots):
    return jnp.clip(table_ref[TABLE_ROWS - 1, a] - group * slots, 0, slots)


def blocks_at(arrays, parts):
    def block(s):
        rows = [arrays[array][pl.ds(pl.multiple_of(first + s * size, 16), size)] for array, first, size in parts]
        return rows[0] if len(rows) == 1 else jnp.concatenate(rows, axis=0)

    return block


def own_kernel(masks, slots, place_ref, table_v, *refs):
    count = len(masks)
    pieces, arrays, (sums_ref, last_ref, stage, table, sem) = refs[:count], refs[count:-5], refs[-5:]
    blocks, _, rows, _ = stage.shape
    before, _, width = sums_ref.shape
    copy = pltpu.make_async_copy(table_v, table, sem)
    copy.start()
    for piece, mask in zip(pieces, masks):
        tiles = piece.shape[1]
        stage[:, pl.ds((place_ref[0] ^ mask) * tiles, tiles)] = piece[...]
    copy.wait()
    places = split(before + 1, slots, width)[0]
    for a, parts in enumerate(places):
        flip = a == before
        total = jnp.zeros((width, blocks * rows) if flip else (blocks * rows, width), jnp.float32)
        live = live_slots(table, a, place_ref[1], slots)
        total = contract(total, table, a, live, slots, stage, blocks_at(arrays, parts), flip)
        if flip:
            last_ref[...] = total
        else:
            sums_ref[a] = total


def head_kernel(slots, place_ref, stage, sums_ref, others, own_ref, soon_ref, late_ref, table_v, table, sem):
    before, both, width = sums_ref.shape
    rows, soon = both // 2, soon_ref.shape[0]
    places, sizes = split(before + 1, slots, width)
    table_v[...] = others[sizes[0]:].astype(jnp.float32).astype(jnp.int32)
    copy = pltpu.make_async_copy(table_v, table, sem)
    copy.start()
    copy.wait()
    for a in range(before):
        live = live_slots(table, a, place_ref[1] ^ 1, slots)
        total = contract(sums_ref[a], table, a, live, slots, stage, blocks_at((others,), places[a]))
        own_ref[a * rows:(a + 1) * rows] = total[:rows]
        cut_at = min(max(soon - a * rows, 0), rows)
        if cut_at > 0:
            soon_ref[a * rows:a * rows + cut_at] = total[rows:rows + cut_at]
        if cut_at < rows:
            first = a * rows + cut_at - soon
            late_ref[first:first + rows - cut_at] = total[rows + cut_at:]


def pick_kernel(a, slots, place_ref, table_v, stage, picked, table, sem):
    blocks, _, rows, depth = stage.shape
    copy = pltpu.make_async_copy(table_v, table, sem)
    copy.start()
    copy.wait()
    live = live_slots(table, a, place_ref[1] ^ 1, slots)
    for s in range(slots):
        block = stage[:, table[a, s]].reshape(blocks * rows, depth)
        picked[:, s * depth:(s + 1) * depth] = jnp.where(s < live, block, jnp.zeros_like(block))


def tail_kernel(slots, n, last_ref, picked, others, own_ref, far_ref):
    size, rows = own_ref.shape
    depth = others.shape[1]
    total = last_ref[n * size:(n + 1) * size]
    for s in range(0, slots, 2):
        some = range(s, min(s + 2, slots))
        weights = jnp.concatenate([others[m * size:(m + 1) * size] for m in some], axis=1)
        sides = picked[:, s * depth:(s + len(some)) * depth]
        total = total + lax.dot_general(weights, sides, (((1,), (1,)), ((), ())), preferred_element_type=jnp.float32)
    own_ref[...] = total[:, :rows]
    far_ref[...] = total[:, rows:]


def join_kernel(*refs):
    own, soon_ref, late_ref, got, out = refs[:1 + PARTS], refs[1 + PARTS], refs[2 + PARTS], refs[3 + PARTS:-1], refs[-1]
    rows, soon = out.shape[0], soon_ref.shape[0]
    before = own[0].shape[0] // rows
    width = out.shape[1] // (before + 1)
    for a in range(before):
        columns = slice(a * width, (a + 1) * width)
        cut_at = min(max(soon - a * rows, 0), rows)
        if cut_at > 0:
            part = slice(a * rows, a * rows + cut_at)
            out[:cut_at, columns] = own[0][part] + soon_ref[part]
        if cut_at < rows:
            first = a * rows + cut_at - soon
            came = late_ref[first:first + rows - cut_at]
            out[cut_at:, columns] = own[0][a * rows + cut_at:(a + 1) * rows] + came
    last = jnp.concatenate([own[1 + n][...] + got[n][...] for n in range(PARTS)], axis=0)
    out[:, before * width:] = jnp.transpose(last)


def on_pairs(amplitudes, tile_counts, tile_lists, integrals, n_vv, n_oo):
    tile_dev, slots, width, depth = integrals.shape
    rows = amplitudes.shape[1]
    tiles = n_vv * tile_dev
    before = tile_dev - 1
    place = jnp.stack([lax.axis_index("vv"), lax.axis_index("oo")]).astype(jnp.int32)

    far = shift(amplitudes, "oo", n_oo, 2)
    *arrays, amplitudes, table = cut(integrals, amplitudes, tile_lists, tile_counts)
    others = [shift(array, "oo", n_oo, 1) for array in arrays]
    block = pl.pallas_call(
        stack_kernel,
        out_shape=jax.ShapeDtypeStruct((2,) + amplitudes.shape, amplitudes.dtype),
        in_specs=[VMEM] * 2,
        out_specs=VMEM,
        compiler_params=pltpu.CompilerParams(vmem_limit_bytes=VMEM_BYTES),
        cost_estimate=pl.CostEstimate(flops=2**20, bytes_accessed=2**19, transcendentals=0),
    )(amplitudes, far)
    pieces, masks = [], []
    for mask in (0, 2, 4, 6):
        piece = shift(block, "vv", n_vv, mask) if mask else block
        pieces += [piece, shift(piece, "vv", n_vv, 1)]
        masks += [mask, mask ^ 1]
    scratch = [pltpu.SMEM(table.shape, table.dtype), pltpu.SemaphoreType.DMA]

    def call(kernel, out, n_smem, n_vmem, scratch, flops):
        return pl.pallas_call(
            kernel,
            out_shape=out,
            in_specs=[SMEM] * n_smem + [VMEM] * n_vmem,
            out_specs=jax.tree.map(lambda _: VMEM, out),
            scratch_shapes=scratch,
            compiler_params=pltpu.CompilerParams(vmem_limit_bytes=VMEM_BYTES),
            cost_estimate=pl.CostEstimate(flops=flops, bytes_accessed=2**21, transcendentals=0),
        )

    def f32(*shape):
        return jax.ShapeDtypeStruct(shape, jnp.float32)

    sums, last, stage = call(
        lambda *refs: own_kernel(masks, slots, *refs),
        (f32(before, 2 * rows, width), f32(width, 2 * rows), jax.ShapeDtypeStruct((2, tiles, rows, depth), far.dtype)),
        1, len(pieces) + 2 + PARTS, scratch, OWN_FLOPS,
    )(place, table, *pieces, *arrays)
    soon = before * rows * SOON // 8
    own, *away, table = call(
        lambda *refs: head_kernel(slots, *refs),
        (
            f32(before * rows, width), f32(soon, width), f32(before * rows - soon, width),
            jax.ShapeDtypeStruct(table.shape, table.dtype),
        ),
        1, 3, scratch, HEAD_FLOPS,
    )(place, stage, sums, others[0])
    picked = call(
        lambda *refs: pick_kernel(before, slots, *refs),
        jax.ShapeDtypeStruct((2 * rows, slots * depth), far.dtype),
        1, 2, scratch, 2**28,
    )(place, table, stage)
    owns, gots = [own], [shift(x, "oo", n_oo, 2) for x in away]
    for n in range(PARTS):
        own, away = call(
            lambda *refs, n=n: tail_kernel(slots, n, *refs), (f32(width // PARTS, rows),) * 2, 0, 3, [], 2**28
        )(last, picked, others[1 + n])
        owns.append(own)
        gots.append(shift(away, "oo", n_oo, 2))
    return call(join_kernel, f32(rows, tile_dev * width), 0, 3 + 2 * PARTS, [], 2**20)(*owns, *gots)


def on_device(amplitudes, tile_counts, tile_lists, integrals, n_vv, n_oo):
    if (n_vv, n_oo) == (8, 4):
        return on_pairs(amplitudes, tile_counts, tile_lists, integrals, n_vv, n_oo)
    slots = tile_lists.shape[1]
    live = jnp.clip(tile_counts - lax.axis_index("oo") * slots, 0, slots)
    rows = lax.all_gather(amplitudes, "oo", axis=0, tiled=False)
    everything = lax.all_gather(rows, "vv", axis=1, tiled=True)
    parts = plain_partials(tile_lists, live, everything, integrals)
    return lax.psum_scatter(parts.reshape(-1, parts.shape[2]), "oo", scatter_dimension=0, tiled=True)


def solution(mesh):
    n_vv, n_oo = mesh.shape["vv"], mesh.shape["oo"]
    placed = (P("vv", "oo", None), P("vv"), P("vv", "oo"), P("vv", "oo", None, None))
    return jax.shard_map(
        lambda *args: on_device(*args, n_vv, n_oo),
        mesh=mesh, in_specs=placed, out_specs=P("oo", "vv"), check_vma=False,
    )
```

```python
import jax
import jax.numpy as jnp
from jax import lax
from jax.experimental import pallas as pl
from jax.experimental.pallas import tpu as pltpu
from jax.sharding import PartitionSpec as P

VMEM_BYTES = 48 * 1024 * 1024
UNROLL = 12
OWN_FLOPS = 3750000000
HEAD_FLOPS = 250000000
SOON = 4
TABLE_ROWS = 16
PARTS = 2
SMEM = pl.BlockSpec(memory_space=pltpu.SMEM)
VMEM = pl.BlockSpec(memory_space=pltpu.VMEM)
ANY = pl.BlockSpec(memory_space=pl.ANY)
HBM = pl.BlockSpec(memory_space=pltpu.HBM)


def shift(value, axis, size, mask):
    return lax.ppermute(value, axis, [(j, j ^ mask) for j in range(size)])


def contract(total, lists_ref, a, live, slots, stage, blocks_of, flip=False):
    blocks, _, rows, depth = stage.shape
    dims = (((1,), (1,)), ((), ()))

    def pair(s):
        sides, weights = [], []
        for slot in (s, s + 1):
            safe = jnp.minimum(slot, slots - 1)
            block = blocks_of(safe)
            sides.append(stage[:, lists_ref[a, safe]].reshape(blocks * rows, depth))
            weights.append(jnp.where(slot < live, block, jnp.zeros_like(block)))
        sides, weights = jnp.concatenate(sides, axis=1), jnp.concatenate(weights, axis=1)
        left, right = (weights, sides) if flip else (sides, weights)
        return lax.dot_general(left, right, dims, preferred_element_type=jnp.float32)

    def step(group, total):
        for offset in range(0, UNROLL, 2):
            total = total + pair(UNROLL * group + offset)
        return total

    return lax.fori_loop(0, (live + UNROLL - 1) // UNROLL, step, total)


def plain_kernel(lists_ref, live_ref, place_ref, piece, integrals_ref, out_ref, stage, sems):
    copy = pltpu.make_async_copy(piece, stage, sems.at[0])
    copy.start()
    copy.wait()
    tile_dev, _, width, _ = integrals_ref.shape
    blocks, _, rows, _ = stage.shape
    for a in range(tile_dev):
        zero = jnp.zeros((blocks * rows, width), jnp.float32)
        total = contract(zero, lists_ref, a, live_ref[a], lists_ref.shape[1], stage, lambda s, a=a: integrals_ref[a, s])
        for k in range(blocks):
            out_ref[k, :, a * width:(a + 1) * width] = total[k * rows:(k + 1) * rows]


def plain_partials(lists, live, everything, integrals):
    blocks, tiles, rows, depth = everything.shape
    tile_dev, _, width, _ = integrals.shape
    return pl.pallas_call(
        plain_kernel,
        out_shape=jax.ShapeDtypeStruct((blocks, rows, tile_dev * width), jnp.float32),
        in_specs=[SMEM] * 3 + [ANY, VMEM],
        out_specs=VMEM,
        scratch_shapes=[pltpu.VMEM((blocks, tiles, rows, depth), everything.dtype), pltpu.SemaphoreType.DMA((1,))],
        compiler_params=pltpu.CompilerParams(vmem_limit_bytes=VMEM_BYTES),
    )(lists, live, jnp.zeros((1,), jnp.int32), everything, integrals)


def split(tile_dev, slots, width):
    size = width // PARTS
    places = [[(0, a * slots * width, width)] for a in range(tile_dev - 1)]
    places.append([(1 + n, 0, size) for n in range(PARTS)])
    return places, [(tile_dev - 1) * slots * width] + [slots * size] * PARTS


def head_cut_kernel(whole, lists, counts, head, table, lists_v, counts_s, sems):
    tile_dev, slots, width, depth = whole.shape
    pairs = [(lists, lists_v), (counts, counts_s)]
    for a in range(tile_dev - 1):
        rows = slots * width
        pairs.append((whole.at[a], head.at[pl.ds(a * rows, rows)].reshape(slots, width, depth)))
    copies = [pltpu.make_async_copy(x, y, sems.at[n]) for n, (x, y) in enumerate(pairs)]
    for copy in copies:
        copy.start()
    for copy in copies[:2]:
        copy.wait()
    lane = lax.broadcasted_iota(jnp.int32, table.shape, 1)
    values = jnp.zeros(table.shape, jnp.int32)
    for a in range(tile_dev):
        values = jnp.where(lane == a, counts_s[a], values)
    table[...] = values
    table[:tile_dev, :slots] = lists_v[...]
    head[(tile_dev - 1) * slots * width:] = table[...].astype(jnp.float32).astype(head.dtype)
    for copy in copies[2:]:
        copy.wait()


def rest_cut_kernel(whole, amplitudes, *refs):
    parts, (amplitudes_out, sems) = refs[:PARTS], refs[PARTS:]
    tile_dev, slots, width, _ = whole.shape
    size = width // PARTS
    pairs = [(amplitudes, amplitudes_out)]
    for n, part in enumerate(parts):
        for s in range(slots):
            pairs.append((whole.at[tile_dev - 1, s, pl.ds(n * size, size)], part.at[pl.ds(s * size, size)]))
    copies = [pltpu.make_async_copy(x, y, sems.at[n]) for n, (x, y) in enumerate(pairs)]
    for copy in copies:
        copy.start()
    for copy in copies:
        copy.wait()


def cut(whole, amplitudes, lists, counts):
    tile_dev, slots, width, depth = whole.shape
    sizes = split(tile_dev, slots, width)[1]
    whole, amplitudes, lists, counts = (
        pltpu.with_memory_space_constraint(x, pltpu.HBM) for x in (whole, amplitudes, lists, counts)
    )
    params = pltpu.CompilerParams(vmem_limit_bytes=VMEM_BYTES)
    head, table = pl.pallas_call(
        head_cut_kernel,
        out_shape=(
            jax.ShapeDtypeStruct((sizes[0] + TABLE_ROWS, depth), whole.dtype),
            jax.ShapeDtypeStruct((TABLE_ROWS, depth), jnp.int32),
        ),
        in_specs=[HBM] * 3,
        out_specs=(VMEM,) * 2,
        scratch_shapes=[
            pltpu.VMEM(lists.shape, lists.dtype),
            pltpu.SMEM(counts.shape, counts.dtype),
            pltpu.SemaphoreType.DMA((1 + tile_dev,)),
        ],
        compiler_params=params,
    )(whole, lists, counts)
    *parts, amplitudes = pl.pallas_call(
        rest_cut_kernel,
        out_shape=(jax.ShapeDtypeStruct((sizes[1], depth), whole.dtype),) * PARTS
        + (jax.ShapeDtypeStruct(amplitudes.shape, amplitudes.dtype),),
        in_specs=[HBM] * 2,
        out_specs=(VMEM,) * (1 + PARTS),
        scratch_shapes=[pltpu.SemaphoreType.DMA((1 + PARTS * slots,))],
        compiler_params=params,
        cost_estimate=pl.CostEstimate(flops=2**20, bytes_accessed=2**19, transcendentals=0),
    )(whole, amplitudes)
    return [head, *parts, amplitudes, table]


def stack_kernel(first, second, out):
    out[0] = first[...]
    out[1] = second[...]


def live_slots(table_ref, a, group, slots):
    return jnp.clip(table_ref[TABLE_ROWS - 1, a] - group * slots, 0, slots)


def blocks_at(arrays, parts):
    def block(s):
        rows = [arrays[array][pl.ds(pl.multiple_of(first + s * size, 16), size)] for array, first, size in parts]
        return rows[0] if len(rows) == 1 else jnp.concatenate(rows, axis=0)

    return block


def own_kernel(masks, slots, place_ref, table_v, *refs):
    count = len(masks)
    pieces, arrays, (sums_ref, last_ref, stage, table, sem) = refs[:count], refs[count:-5], refs[-5:]
    blocks, _, rows, _ = stage.shape
    before, _, width = sums_ref.shape
    copy = pltpu.make_async_copy(table_v, table, sem)
    copy.start()
    for piece, mask in zip(pieces, masks):
        tiles = piece.shape[1]
        stage[:, pl.ds((place_ref[0] ^ mask) * tiles, tiles)] = piece[...]
    copy.wait()
    places = split(before + 1, slots, width)[0]
    for a, parts in enumerate(places):
        flip = a == before
        total = jnp.zeros((width, blocks * rows) if flip else (blocks * rows, width), jnp.float32)
        live = live_slots(table, a, place_ref[1], slots)
        total = contract(total, table, a, live, slots, stage, blocks_at(arrays, parts), flip)
        if flip:
            last_ref[...] = total
        else:
            sums_ref[a] = total


def head_kernel(slots, place_ref, stage, sums_ref, others, own_ref, soon_ref, late_ref, table_v, table, sem):
    before, both, width = sums_ref.shape
    rows, soon = both // 2, soon_ref.shape[0]
    places, sizes = split(before + 1, slots, width)
    table_v[...] = others[sizes[0]:].astype(jnp.float32).astype(jnp.int32)
    copy = pltpu.make_async_copy(table_v, table, sem)
    copy.start()
    copy.wait()
    for a in range(before):
        live = live_slots(table, a, place_ref[1] ^ 1, slots)
        total = contract(sums_ref[a], table, a, live, slots, stage, blocks_at((others,), places[a]))
        own_ref[a * rows:(a + 1) * rows] = total[:rows]
        cut_at = min(max(soon - a * rows, 0), rows)
        if cut_at > 0:
            soon_ref[a * rows:a * rows + cut_at] = total[rows:rows + cut_at]
        if cut_at < rows:
            first = a * rows + cut_at - soon
            late_ref[first:first + rows - cut_at] = total[rows + cut_at:]


def pick_kernel(a, slots, place_ref, table_v, stage, picked, table, sem):
    blocks, _, rows, depth = stage.shape
    copy = pltpu.make_async_copy(table_v, table, sem)
    copy.start()
    copy.wait()
    live = live_slots(table, a, place_ref[1] ^ 1, slots)
    for s in range(slots):
        block = stage[:, table[a, s]].reshape(blocks * rows, depth)
        picked[:, s * depth:(s + 1) * depth] = jnp.where(s < live, block, jnp.zeros_like(block))


def tail_kernel(slots, n, last_ref, picked, others, own_ref, far_ref):
    size, rows = own_ref.shape
    depth = others.shape[1]
    total = last_ref[n * size:(n + 1) * size]
    for s in range(0, slots, 2):
        some = range(s, min(s + 2, slots))
        weights = jnp.concatenate([others[m * size:(m + 1) * size] for m in some], axis=1)
        sides = picked[:, s * depth:(s + len(some)) * depth]
        total = total + lax.dot_general(weights, sides, (((1,), (1,)), ((), ())), preferred_element_type=jnp.float32)
    own_ref[...] = total[:, :rows]
    far_ref[...] = total[:, rows:]


def join_kernel(*refs):
    own, soon_ref, late_ref, got, out = refs[:1 + PARTS], refs[1 + PARTS], refs[2 + PARTS], refs[3 + PARTS:-1], refs[-1]
    rows, soon = out.shape[0], soon_ref.shape[0]
    before = own[0].shape[0] // rows
    width = out.shape[1] // (before + 1)
    for a in range(before):
        columns = slice(a * width, (a + 1) * width)
        cut_at = min(max(soon - a * rows, 0), rows)
        if cut_at > 0:
            part = slice(a * rows, a * rows + cut_at)
            out[:cut_at, columns] = own[0][part] + soon_ref[part]
        if cut_at < rows:
            first = a * rows + cut_at - soon
            came = late_ref[first:first + rows - cut_at]
            out[cut_at:, columns] = own[0][a * rows + cut_at:(a + 1) * rows] + came
    last = jnp.concatenate([own[1 + n][...] + got[n][...] for n in range(PARTS)], axis=0)
    out[:, before * width:] = jnp.transpose(last)


def on_pairs(amplitudes, tile_counts, tile_lists, integrals, n_vv, n_oo):
    tile_dev, slots, width, depth = integrals.shape
    rows = amplitudes.shape[1]
    tiles = n_vv * tile_dev
    before = tile_dev - 1
    place = jnp.stack([lax.axis_index("vv"), lax.axis_index("oo")]).astype(jnp.int32)

    far = shift(amplitudes, "oo", n_oo, 2)
    *arrays, amplitudes, table = cut(integrals, amplitudes, tile_lists, tile_counts)
    others = [shift(array, "oo", n_oo, 1) for array in arrays]
    block = pl.pallas_call(
        stack_kernel,
        out_shape=jax.ShapeDtypeStruct((2,) + amplitudes.shape, amplitudes.dtype),
        in_specs=[VMEM] * 2,
        out_specs=VMEM,
        compiler_params=pltpu.CompilerParams(vmem_limit_bytes=VMEM_BYTES),
        cost_estimate=pl.CostEstimate(flops=2**20, bytes_accessed=2**19, transcendentals=0),
    )(amplitudes, far)
    pieces, masks = [], []
    for mask in (0, 2, 4, 6):
        piece = shift(block, "vv", n_vv, mask) if mask else block
        pieces += [piece, shift(piece, "vv", n_vv, 1)]
        masks += [mask, mask ^ 1]
    scratch = [pltpu.SMEM(table.shape, table.dtype), pltpu.SemaphoreType.DMA]

    def call(kernel, out, n_smem, n_vmem, scratch, flops):
        return pl.pallas_call(
            kernel,
            out_shape=out,
            in_specs=[SMEM] * n_smem + [VMEM] * n_vmem,
            out_specs=jax.tree.map(lambda _: VMEM, out),
            scratch_shapes=scratch,
            compiler_params=pltpu.CompilerParams(vmem_limit_bytes=VMEM_BYTES),
            cost_estimate=pl.CostEstimate(flops=flops, bytes_accessed=2**21, transcendentals=0),
        )

    def f32(*shape):
        return jax.ShapeDtypeStruct(shape, jnp.float32)

    sums, last, stage = call(
        lambda *refs: own_kernel(masks, slots, *refs),
        (f32(before, 2 * rows, width), f32(width, 2 * rows), jax.ShapeDtypeStruct((2, tiles, rows, depth), far.dtype)),
        1, len(pieces) + 2 + PARTS, scratch, OWN_FLOPS,
    )(place, table, *pieces, *arrays)
    soon = before * rows * SOON // 8
    own, *away, table = call(
        lambda *refs: head_kernel(slots, *refs),
        (
            f32(before * rows, width), f32(soon, width), f32(before * rows - soon, width),
            jax.ShapeDtypeStruct(table.shape, table.dtype),
        ),
        1, 3, scratch, HEAD_FLOPS,
    )(place, stage, sums, others[0])
    picked = call(
        lambda *refs: pick_kernel(before, slots, *refs),
        jax.ShapeDtypeStruct((2 * rows, slots * depth), far.dtype),
        1, 2, scratch, 2**28,
    )(place, table, stage)
    owns, gots = [own], [shift(x, "oo", n_oo, 2) for x in away]
    for n in range(PARTS):
        own, away = call(
            lambda *refs, n=n: tail_kernel(slots, n, *refs), (f32(width // PARTS, rows),) * 2, 0, 3, [], 2**28
        )(last, picked, others[1 + n])
        owns.append(own)
        gots.append(shift(away, "oo", n_oo, 2))
    return call(join_kernel, f32(rows, tile_dev * width), 0, 3 + 2 * PARTS, [], 2**20)(*owns, *gots)


def on_device(amplitudes, tile_counts, tile_lists, integrals, n_vv, n_oo):
    if (n_vv, n_oo) == (8, 4):
        return on_pairs(amplitudes, tile_counts, tile_lists, integrals, n_vv, n_oo)
    slots = tile_lists.shape[1]
    live = jnp.clip(tile_counts - lax.axis_index("oo") * slots, 0, slots)
    rows = lax.all_gather(amplitudes, "oo", axis=0, tiled=False)
    everything = lax.all_gather(rows, "vv", axis=1, tiled=True)
    parts = plain_partials(tile_lists, live, everything, integrals)
    return lax.psum_scatter(parts.reshape(-1, parts.shape[2]), "oo", scatter_dimension=0, tiled=True)


def solution(mesh):
    n_vv, n_oo = mesh.shape["vv"], mesh.shape["oo"]
    placed = (P("vv", "oo", None), P("vv"), P("vv", "oo"), P("vv", "oo", None, None))
    return jax.shard_map(
        lambda *args: on_device(*args, n_vv, n_oo),
        mesh=mesh, in_specs=placed, out_specs=P("oo", "vv"), check_vma=False,
    )
```

```python
import jax
import jax.numpy as jnp
from jax import lax
from jax.experimental import pallas as pl
from jax.experimental.pallas import tpu as pltpu
from jax.sharding import PartitionSpec as P

VMEM_BYTES = 48 * 1024 * 1024
UNROLL = 12
OWN_FLOPS = 3750000000
HEAD_FLOPS = 250000000
SOON = 4
TABLE_ROWS = 16
PARTS = 2
SMEM = pl.BlockSpec(memory_space=pltpu.SMEM)
VMEM = pl.BlockSpec(memory_space=pltpu.VMEM)
ANY = pl.BlockSpec(memory_space=pl.ANY)
HBM = pl.BlockSpec(memory_space=pltpu.HBM)


def shift(value, axis, size, mask):
    return lax.ppermute(value, axis, [(j, j ^ mask) for j in range(size)])


def contract(total, lists_ref, a, live, slots, stage, blocks_of, flip=False):
    blocks, _, rows, depth = stage.shape
    dims = (((1,), (1,)), ((), ()))

    def pair(s):
        sides, weights = [], []
        for slot in (s, s + 1):
            safe = jnp.minimum(slot, slots - 1)
            block = blocks_of(safe)
            sides.append(stage[:, lists_ref[a, safe]].reshape(blocks * rows, depth))
            weights.append(jnp.where(slot < live, block, jnp.zeros_like(block)))
        sides, weights = jnp.concatenate(sides, axis=1), jnp.concatenate(weights, axis=1)
        left, right = (weights, sides) if flip else (sides, weights)
        return lax.dot_general(left, right, dims, preferred_element_type=jnp.float32)

    def step(group, total):
        for offset in range(0, UNROLL, 2):
            total = total + pair(UNROLL * group + offset)
        return total

    return lax.fori_loop(0, (live + UNROLL - 1) // UNROLL, step, total)


def plain_kernel(lists_ref, live_ref, place_ref, piece, integrals_ref, out_ref, stage, sems):
    copy = pltpu.make_async_copy(piece, stage, sems.at[0])
    copy.start()
    copy.wait()
    tile_dev, _, width, _ = integrals_ref.shape
    blocks, _, rows, _ = stage.shape
    for a in range(tile_dev):
        zero = jnp.zeros((blocks * rows, width), jnp.float32)
        total = contract(zero, lists_ref, a, live_ref[a], lists_ref.shape[1], stage, lambda s, a=a: integrals_ref[a, s])
        for k in range(blocks):
            out_ref[k, :, a * width:(a + 1) * width] = total[k * rows:(k + 1) * rows]


def plain_partials(lists, live, everything, integrals):
    blocks, tiles, rows, depth = everything.shape
    tile_dev, _, width, _ = integrals.shape
    return pl.pallas_call(
        plain_kernel,
        out_shape=jax.ShapeDtypeStruct((blocks, rows, tile_dev * width), jnp.float32),
        in_specs=[SMEM] * 3 + [ANY, VMEM],
        out_specs=VMEM,
        scratch_shapes=[pltpu.VMEM((blocks, tiles, rows, depth), everything.dtype), pltpu.SemaphoreType.DMA((1,))],
        compiler_params=pltpu.CompilerParams(vmem_limit_bytes=VMEM_BYTES),
    )(lists, live, jnp.zeros((1,), jnp.int32), everything, integrals)


def split(tile_dev, slots, width):
    size = width // PARTS
    places = [[(0, a * slots * width, width)] for a in range(tile_dev - 1)]
    places.append([(1 + n, 0, size) for n in range(PARTS)])
    return places, [(tile_dev - 1) * slots * width] + [slots * size] * PARTS


def head_cut_kernel(whole, lists, counts, head, table, lists_v, counts_s, sems):
    tile_dev, slots, width, depth = whole.shape
    pairs = [(lists, lists_v), (counts, counts_s)]
    for a in range(tile_dev - 1):
        rows = slots * width
        pairs.append((whole.at[a], head.at[pl.ds(a * rows, rows)].reshape(slots, width, depth)))
    copies = [pltpu.make_async_copy(x, y, sems.at[n]) for n, (x, y) in enumerate(pairs)]
    for copy in copies:
        copy.start()
    for copy in copies[:2]:
        copy.wait()
    lane = lax.broadcasted_iota(jnp.int32, table.shape, 1)
    values = jnp.zeros(table.shape, jnp.int32)
    for a in range(tile_dev):
        values = jnp.where(lane == a, counts_s[a], values)
    table[...] = values
    table[:tile_dev, :slots] = lists_v[...]
    head[(tile_dev - 1) * slots * width:] = table[...].astype(jnp.float32).astype(head.dtype)
    for copy in copies[2:]:
        copy.wait()


def rest_cut_kernel(whole, amplitudes, *refs):
    parts, (amplitudes_out, sems) = refs[:PARTS], refs[PARTS:]
    tile_dev, slots, width, _ = whole.shape
    size = width // PARTS
    pairs = [(amplitudes, amplitudes_out)]
    for n, part in enumerate(parts):
        for s in range(slots):
            pairs.append((whole.at[tile_dev - 1, s, pl.ds(n * size, size)], part.at[pl.ds(s * size, size)]))
    copies = [pltpu.make_async_copy(x, y, sems.at[n]) for n, (x, y) in enumerate(pairs)]
    for copy in copies:
        copy.start()
    for copy in copies:
        copy.wait()


def cut(whole, amplitudes, lists, counts):
    tile_dev, slots, width, depth = whole.shape
    sizes = split(tile_dev, slots, width)[1]
    whole, amplitudes, lists, counts = (
        pltpu.with_memory_space_constraint(x, pltpu.HBM) for x in (whole, amplitudes, lists, counts)
    )
    params = pltpu.CompilerParams(vmem_limit_bytes=VMEM_BYTES)
    head, table = pl.pallas_call(
        head_cut_kernel,
        out_shape=(
            jax.ShapeDtypeStruct((sizes[0] + TABLE_ROWS, depth), whole.dtype),
            jax.ShapeDtypeStruct((TABLE_ROWS, depth), jnp.int32),
        ),
        in_specs=[HBM] * 3,
        out_specs=(VMEM,) * 2,
        scratch_shapes=[
            pltpu.VMEM(lists.shape, lists.dtype),
            pltpu.SMEM(counts.shape, counts.dtype),
            pltpu.SemaphoreType.DMA((1 + tile_dev,)),
        ],
        compiler_params=params,
    )(whole, lists, counts)
    *parts, amplitudes = pl.pallas_call(
        rest_cut_kernel,
        out_shape=(jax.ShapeDtypeStruct((sizes[1], depth), whole.dtype),) * PARTS
        + (jax.ShapeDtypeStruct(amplitudes.shape, amplitudes.dtype),),
        in_specs=[HBM] * 2,
        out_specs=(VMEM,) * (1 + PARTS),
        scratch_shapes=[pltpu.SemaphoreType.DMA((1 + PARTS * slots,))],
        compiler_params=params,
        cost_estimate=pl.CostEstimate(flops=2**20, bytes_accessed=2**19, transcendentals=0),
    )(whole, amplitudes)
    return [head, *parts, amplitudes, table]


def stack_kernel(first, second, out):
    out[0] = first[...]
    out[1] = second[...]


def live_slots(table_ref, a, group, slots):
    return jnp.clip(table_ref[TABLE_ROWS - 1, a] - group * slots, 0, slots)


def blocks_at(arrays, parts):
    def block(s):
        rows = [arrays[array][pl.ds(pl.multiple_of(first + s * size, 16), size)] for array, first, size in parts]
        return rows[0] if len(rows) == 1 else jnp.concatenate(rows, axis=0)

    return block


def own_kernel(masks, slots, place_ref, table_v, *refs):
    count = len(masks)
    pieces, arrays, (sums_ref, last_ref, stage, table, sem) = refs[:count], refs[count:-5], refs[-5:]
    blocks, _, rows, _ = stage.shape
    before, _, width = sums_ref.shape
    copy = pltpu.make_async_copy(table_v, table, sem)
    copy.start()
    for piece, mask in zip(pieces, masks):
        tiles = piece.shape[1]
        stage[:, pl.ds((place_ref[0] ^ mask) * tiles, tiles)] = piece[...]
    copy.wait()
    places = split(before + 1, slots, width)[0]
    for a, parts in enumerate(places):
        flip = a == before
        total = jnp.zeros((width, blocks * rows) if flip else (blocks * rows, width), jnp.float32)
        live = live_slots(table, a, place_ref[1], slots)
        total = contract(total, table, a, live, slots, stage, blocks_at(arrays, parts), flip)
        if flip:
            last_ref[...] = total
        else:
            sums_ref[a] = total


def head_kernel(slots, place_ref, stage, sums_ref, others, own_ref, soon_ref, late_ref, table_v, table, sem):
    before, both, width = sums_ref.shape
    rows, soon = both // 2, soon_ref.shape[0]
    places, sizes = split(before + 1, slots, width)
    table_v[...] = others[sizes[0]:].astype(jnp.float32).astype(jnp.int32)
    copy = pltpu.make_async_copy(table_v, table, sem)
    copy.start()
    copy.wait()
    for a in range(before):
        live = live_slots(table, a, place_ref[1] ^ 1, slots)
        total = contract(sums_ref[a], table, a, live, slots, stage, blocks_at((others,), places[a]))
        own_ref[a * rows:(a + 1) * rows] = total[:rows]
        cut_at = min(max(soon - a * rows, 0), rows)
        if cut_at > 0:
            soon_ref[a * rows:a * rows + cut_at] = total[rows:rows + cut_at]
        if cut_at < rows:
            first = a * rows + cut_at - soon
            late_ref[first:first + rows - cut_at] = total[rows + cut_at:]


def pick_kernel(a, slots, place_ref, table_v, stage, picked, table, sem):
    blocks, _, rows, depth = stage.shape
    copy = pltpu.make_async_copy(table_v, table, sem)
    copy.start()
    copy.wait()
    live = live_slots(table, a, place_ref[1] ^ 1, slots)
    for s in range(slots):
        block = stage[:, table[a, s]].reshape(blocks * rows, depth)
        picked[:, s * depth:(s + 1) * depth] = jnp.where(s < live, block, jnp.zeros_like(block))


def tail_kernel(slots, n, last_ref, picked, others, own_ref, far_ref):
    size, rows = own_ref.shape
    depth = others.shape[1]
    total = last_ref[n * size:(n + 1) * size]
    for s in range(0, slots, 2):
        some = range(s, min(s + 2, slots))
        weights = jnp.concatenate([others[m * size:(m + 1) * size] for m in some], axis=1)
        sides = picked[:, s * depth:(s + len(some)) * depth]
        total = total + lax.dot_general(weights, sides, (((1,), (1,)), ((), ())), preferred_element_type=jnp.float32)
    own_ref[...] = total[:, :rows]
    far_ref[...] = total[:, rows:]


def join_kernel(*refs):
    own, soon_ref, late_ref, got, out = refs[:1 + PARTS], refs[1 + PARTS], refs[2 + PARTS], refs[3 + PARTS:-1], refs[-1]
    rows, soon = out.shape[0], soon_ref.shape[0]
    before = own[0].shape[0] // rows
    width = out.shape[1] // (before + 1)
    for a in range(before):
        columns = slice(a * width, (a + 1) * width)
        cut_at = min(max(soon - a * rows, 0), rows)
        if cut_at > 0:
            part = slice(a * rows, a * rows + cut_at)
            out[:cut_at, columns] = own[0][part] + soon_ref[part]
        if cut_at < rows:
            first = a * rows + cut_at - soon
            came = late_ref[first:first + rows - cut_at]
            out[cut_at:, columns] = own[0][a * rows + cut_at:(a + 1) * rows] + came
    last = jnp.concatenate([own[1 + n][...] + got[n][...] for n in range(PARTS)], axis=0)
    out[:, before * width:] = jnp.transpose(last)


def on_pairs(amplitudes, tile_counts, tile_lists, integrals, n_vv, n_oo):
    tile_dev, slots, width, depth = integrals.shape
    rows = amplitudes.shape[1]
    tiles = n_vv * tile_dev
    before = tile_dev - 1
    place = jnp.stack([lax.axis_index("vv"), lax.axis_index("oo")]).astype(jnp.int32)

    far = shift(amplitudes, "oo", n_oo, 2)
    *arrays, amplitudes, table = cut(integrals, amplitudes, tile_lists, tile_counts)
    others = [shift(array, "oo", n_oo, 1) for array in arrays]
    block = pl.pallas_call(
        stack_kernel,
        out_shape=jax.ShapeDtypeStruct((2,) + amplitudes.shape, amplitudes.dtype),
        in_specs=[VMEM] * 2,
        out_specs=VMEM,
        compiler_params=pltpu.CompilerParams(vmem_limit_bytes=VMEM_BYTES),
        cost_estimate=pl.CostEstimate(flops=2**20, bytes_accessed=2**19, transcendentals=0),
    )(amplitudes, far)
    pieces, masks = [], []
    for mask in (0, 2, 4, 6):
        piece = shift(block, "vv", n_vv, mask) if mask else block
        pieces += [piece, shift(piece, "vv", n_vv, 1)]
        masks += [mask, mask ^ 1]
    scratch = [pltpu.SMEM(table.shape, table.dtype), pltpu.SemaphoreType.DMA]

    def call(kernel, out, n_smem, n_vmem, scratch, flops):
        return pl.pallas_call(
            kernel,
            out_shape=out,
            in_specs=[SMEM] * n_smem + [VMEM] * n_vmem,
            out_specs=jax.tree.map(lambda _: VMEM, out),
            scratch_shapes=scratch,
            compiler_params=pltpu.CompilerParams(vmem_limit_bytes=VMEM_BYTES),
            cost_estimate=pl.CostEstimate(flops=flops, bytes_accessed=2**21, transcendentals=0),
        )

    def f32(*shape):
        return jax.ShapeDtypeStruct(shape, jnp.float32)

    sums, last, stage = call(
        lambda *refs: own_kernel(masks, slots, *refs),
        (f32(before, 2 * rows, width), f32(width, 2 * rows), jax.ShapeDtypeStruct((2, tiles, rows, depth), far.dtype)),
        1, len(pieces) + 2 + PARTS, scratch, OWN_FLOPS,
    )(place, table, *pieces, *arrays)
    soon = before * rows * SOON // 8
    own, *away, table = call(
        lambda *refs: head_kernel(slots, *refs),
        (
            f32(before * rows, width), f32(soon, width), f32(before * rows - soon, width),
            jax.ShapeDtypeStruct(table.shape, table.dtype),
        ),
        1, 3, scratch, HEAD_FLOPS,
    )(place, stage, sums, others[0])
    picked = call(
        lambda *refs: pick_kernel(before, slots, *refs),
        jax.ShapeDtypeStruct((2 * rows, slots * depth), far.dtype),
        1, 2, scratch, 2**28,
    )(place, table, stage)
    soon, late = away
    late, picked = lax.optimization_barrier((late, picked))
    owns, gots = [own], [shift(x, "oo", n_oo, 2) for x in (soon, late)]
    for n in range(PARTS):
        own, away = call(
            lambda *refs, n=n: tail_kernel(slots, n, *refs), (f32(width // PARTS, rows),) * 2, 0, 3, [], 2**28
        )(last, picked, others[1 + n])
        owns.append(own)
        gots.append(shift(away, "oo", n_oo, 2))
    return call(join_kernel, f32(rows, tile_dev * width), 0, 3 + 2 * PARTS, [], 2**20)(*owns, *gots)


def on_device(amplitudes, tile_counts, tile_lists, integrals, n_vv, n_oo):
    if (n_vv, n_oo) == (8, 4):
        return on_pairs(amplitudes, tile_counts, tile_lists, integrals, n_vv, n_oo)
    slots = tile_lists.shape[1]
    live = jnp.clip(tile_counts - lax.axis_index("oo") * slots, 0, slots)
    rows = lax.all_gather(amplitudes, "oo", axis=0, tiled=False)
    everything = lax.all_gather(rows, "vv", axis=1, tiled=True)
    parts = plain_partials(tile_lists, live, everything, integrals)
    return lax.psum_scatter(parts.reshape(-1, parts.shape[2]), "oo", scatter_dimension=0, tiled=True)


def solution(mesh):
    n_vv, n_oo = mesh.shape["vv"], mesh.shape["oo"]
    placed = (P("vv", "oo", None), P("vv"), P("vv", "oo"), P("vv", "oo", None, None))
    return jax.shard_map(
        lambda *args: on_device(*args, n_vv, n_oo),
        mesh=mesh, in_specs=placed, out_specs=P("oo", "vv"), check_vma=False,
    )
```

```python
import jax
import jax.numpy as jnp
from jax import lax
from jax.experimental import pallas as pl
from jax.experimental.pallas import tpu as pltpu
from jax.sharding import PartitionSpec as P

VMEM_BYTES = 48 * 1024 * 1024
UNROLL = 12
OWN_FLOPS = 3750000000
HEAD_FLOPS = 250000000
SOON = 5
TABLE_ROWS = 16
PARTS = 2
SMEM = pl.BlockSpec(memory_space=pltpu.SMEM)
VMEM = pl.BlockSpec(memory_space=pltpu.VMEM)
ANY = pl.BlockSpec(memory_space=pl.ANY)
HBM = pl.BlockSpec(memory_space=pltpu.HBM)


def shift(value, axis, size, mask):
    return lax.ppermute(value, axis, [(j, j ^ mask) for j in range(size)])


def contract(total, lists_ref, a, live, slots, stage, blocks_of, flip=False):
    blocks, _, rows, depth = stage.shape
    dims = (((1,), (1,)), ((), ()))

    def pair(s):
        sides, weights = [], []
        for slot in (s, s + 1):
            safe = jnp.minimum(slot, slots - 1)
            block = blocks_of(safe)
            sides.append(stage[:, lists_ref[a, safe]].reshape(blocks * rows, depth))
            weights.append(jnp.where(slot < live, block, jnp.zeros_like(block)))
        sides, weights = jnp.concatenate(sides, axis=1), jnp.concatenate(weights, axis=1)
        left, right = (weights, sides) if flip else (sides, weights)
        return lax.dot_general(left, right, dims, preferred_element_type=jnp.float32)

    def step(group, total):
        for offset in range(0, UNROLL, 2):
            total = total + pair(UNROLL * group + offset)
        return total

    return lax.fori_loop(0, (live + UNROLL - 1) // UNROLL, step, total)


def plain_kernel(lists_ref, live_ref, place_ref, piece, integrals_ref, out_ref, stage, sems):
    copy = pltpu.make_async_copy(piece, stage, sems.at[0])
    copy.start()
    copy.wait()
    tile_dev, _, width, _ = integrals_ref.shape
    blocks, _, rows, _ = stage.shape
    for a in range(tile_dev):
        zero = jnp.zeros((blocks * rows, width), jnp.float32)
        total = contract(zero, lists_ref, a, live_ref[a], lists_ref.shape[1], stage, lambda s, a=a: integrals_ref[a, s])
        for k in range(blocks):
            out_ref[k, :, a * width:(a + 1) * width] = total[k * rows:(k + 1) * rows]


def plain_partials(lists, live, everything, integrals):
    blocks, tiles, rows, depth = everything.shape
    tile_dev, _, width, _ = integrals.shape
    return pl.pallas_call(
        plain_kernel,
        out_shape=jax.ShapeDtypeStruct((blocks, rows, tile_dev * width), jnp.float32),
        in_specs=[SMEM] * 3 + [ANY, VMEM],
        out_specs=VMEM,
        scratch_shapes=[pltpu.VMEM((blocks, tiles, rows, depth), everything.dtype), pltpu.SemaphoreType.DMA((1,))],
        compiler_params=pltpu.CompilerParams(vmem_limit_bytes=VMEM_BYTES),
    )(lists, live, jnp.zeros((1,), jnp.int32), everything, integrals)


def split(tile_dev, slots, width):
    size = width // PARTS
    places = [[(0, a * slots * width, width)] for a in range(tile_dev - 1)]
    places.append([(1 + n, 0, size) for n in range(PARTS)])
    return places, [(tile_dev - 1) * slots * width] + [slots * size] * PARTS


def head_cut_kernel(whole, lists, counts, head, table, lists_v, counts_s, sems):
    tile_dev, slots, width, depth = whole.shape
    pairs = [(lists, lists_v), (counts, counts_s)]
    for a in range(tile_dev - 1):
        rows = slots * width
        pairs.append((whole.at[a], head.at[pl.ds(a * rows, rows)].reshape(slots, width, depth)))
    copies = [pltpu.make_async_copy(x, y, sems.at[n]) for n, (x, y) in enumerate(pairs)]
    for copy in copies:
        copy.start()
    for copy in copies[:2]:
        copy.wait()
    lane = lax.broadcasted_iota(jnp.int32, table.shape, 1)
    values = jnp.zeros(table.shape, jnp.int32)
    for a in range(tile_dev):
        values = jnp.where(lane == a, counts_s[a], values)
    table[...] = values
    table[:tile_dev, :slots] = lists_v[...]
    head[(tile_dev - 1) * slots * width:] = table[...].astype(jnp.float32).astype(head.dtype)
    for copy in copies[2:]:
        copy.wait()


def rest_cut_kernel(whole, amplitudes, *refs):
    parts, (amplitudes_out, sems) = refs[:PARTS], refs[PARTS:]
    tile_dev, slots, width, _ = whole.shape
    size = width // PARTS
    pairs = [(amplitudes, amplitudes_out)]
    for n, part in enumerate(parts):
        for s in range(slots):
            pairs.append((whole.at[tile_dev - 1, s, pl.ds(n * size, size)], part.at[pl.ds(s * size, size)]))
    copies = [pltpu.make_async_copy(x, y, sems.at[n]) for n, (x, y) in enumerate(pairs)]
    for copy in copies:
        copy.start()
    for copy in copies:
        copy.wait()


def cut(whole, amplitudes, lists, counts):
    tile_dev, slots, width, depth = whole.shape
    sizes = split(tile_dev, slots, width)[1]
    whole, amplitudes, lists, counts = (
        pltpu.with_memory_space_constraint(x, pltpu.HBM) for x in (whole, amplitudes, lists, counts)
    )
    params = pltpu.CompilerParams(vmem_limit_bytes=VMEM_BYTES)
    head, table = pl.pallas_call(
        head_cut_kernel,
        out_shape=(
            jax.ShapeDtypeStruct((sizes[0] + TABLE_ROWS, depth), whole.dtype),
            jax.ShapeDtypeStruct((TABLE_ROWS, depth), jnp.int32),
        ),
        in_specs=[HBM] * 3,
        out_specs=(VMEM,) * 2,
        scratch_shapes=[
            pltpu.VMEM(lists.shape, lists.dtype),
            pltpu.SMEM(counts.shape, counts.dtype),
            pltpu.SemaphoreType.DMA((1 + tile_dev,)),
        ],
        compiler_params=params,
    )(whole, lists, counts)
    *parts, amplitudes = pl.pallas_call(
        rest_cut_kernel,
        out_shape=(jax.ShapeDtypeStruct((sizes[1], depth), whole.dtype),) * PARTS
        + (jax.ShapeDtypeStruct(amplitudes.shape, amplitudes.dtype),),
        in_specs=[HBM] * 2,
        out_specs=(VMEM,) * (1 + PARTS),
        scratch_shapes=[pltpu.SemaphoreType.DMA((1 + PARTS * slots,))],
        compiler_params=params,
        cost_estimate=pl.CostEstimate(flops=2**20, bytes_accessed=2**19, transcendentals=0),
    )(whole, amplitudes)
    return [head, *parts, amplitudes, table]


def stack_kernel(first, second, out):
    out[0] = first[...]
    out[1] = second[...]


def live_slots(table_ref, a, group, slots):
    return jnp.clip(table_ref[TABLE_ROWS - 1, a] - group * slots, 0, slots)


def blocks_at(arrays, parts):
    def block(s):
        rows = [arrays[array][pl.ds(pl.multiple_of(first + s * size, 16), size)] for array, first, size in parts]
        return rows[0] if len(rows) == 1 else jnp.concatenate(rows, axis=0)

    return block


def own_kernel(masks, slots, place_ref, table_v, *refs):
    count = len(masks)
    pieces, arrays, (sums_ref, last_ref, stage, table, sem) = refs[:count], refs[count:-5], refs[-5:]
    blocks, _, rows, _ = stage.shape
    before, _, width = sums_ref.shape
    copy = pltpu.make_async_copy(table_v, table, sem)
    copy.start()
    for piece, mask in zip(pieces, masks):
        tiles = piece.shape[1]
        stage[:, pl.ds((place_ref[0] ^ mask) * tiles, tiles)] = piece[...]
    copy.wait()
    places = split(before + 1, slots, width)[0]
    for a, parts in enumerate(places):
        flip = a == before
        total = jnp.zeros((width, blocks * rows) if flip else (blocks * rows, width), jnp.float32)
        live = live_slots(table, a, place_ref[1], slots)
        total = contract(total, table, a, live, slots, stage, blocks_at(arrays, parts), flip)
        if flip:
            last_ref[...] = total
        else:
            sums_ref[a] = total


def head_kernel(slots, place_ref, stage, sums_ref, others, own_ref, soon_ref, late_ref, table_v, table, sem):
    before, both, width = sums_ref.shape
    rows, soon = both // 2, soon_ref.shape[0]
    places, sizes = split(before + 1, slots, width)
    table_v[...] = others[sizes[0]:].astype(jnp.float32).astype(jnp.int32)
    copy = pltpu.make_async_copy(table_v, table, sem)
    copy.start()
    copy.wait()
    for a in range(before):
        live = live_slots(table, a, place_ref[1] ^ 1, slots)
        total = contract(sums_ref[a], table, a, live, slots, stage, blocks_at((others,), places[a]))
        own_ref[a * rows:(a + 1) * rows] = total[:rows]
        cut_at = min(max(soon - a * rows, 0), rows)
        if cut_at > 0:
            soon_ref[a * rows:a * rows + cut_at] = total[rows:rows + cut_at]
        if cut_at < rows:
            first = a * rows + cut_at - soon
            late_ref[first:first + rows - cut_at] = total[rows + cut_at:]


def pick_kernel(a, slots, place_ref, table_v, stage, picked, table, sem):
    blocks, _, rows, depth = stage.shape
    copy = pltpu.make_async_copy(table_v, table, sem)
    copy.start()
    copy.wait()
    live = live_slots(table, a, place_ref[1] ^ 1, slots)
    for s in range(slots):
        block = stage[:, table[a, s]].reshape(blocks * rows, depth)
        picked[:, s * depth:(s + 1) * depth] = jnp.where(s < live, block, jnp.zeros_like(block))


def tail_kernel(slots, n, last_ref, picked, others, own_ref, far_ref):
    size, rows = own_ref.shape
    depth = others.shape[1]
    total = last_ref[n * size:(n + 1) * size]
    for s in range(0, slots, 2):
        some = range(s, min(s + 2, slots))
        weights = jnp.concatenate([others[m * size:(m + 1) * size] for m in some], axis=1)
        sides = picked[:, s * depth:(s + len(some)) * depth]
        total = total + lax.dot_general(weights, sides, (((1,), (1,)), ((), ())), preferred_element_type=jnp.float32)
    own_ref[...] = total[:, :rows]
    far_ref[...] = total[:, rows:]


def join_kernel(*refs):
    own, soon_ref, late_ref, got, out = refs[:1 + PARTS], refs[1 + PARTS], refs[2 + PARTS], refs[3 + PARTS:-1], refs[-1]
    rows, soon = out.shape[0], soon_ref.shape[0]
    before = own[0].shape[0] // rows
    width = out.shape[1] // (before + 1)
    for a in range(before):
        columns = slice(a * width, (a + 1) * width)
        cut_at = min(max(soon - a * rows, 0), rows)
        if cut_at > 0:
            part = slice(a * rows, a * rows + cut_at)
            out[:cut_at, columns] = own[0][part] + soon_ref[part]
        if cut_at < rows:
            first = a * rows + cut_at - soon
            came = late_ref[first:first + rows - cut_at]
            out[cut_at:, columns] = own[0][a * rows + cut_at:(a + 1) * rows] + came
    last = jnp.concatenate([own[1 + n][...] + got[n][...] for n in range(PARTS)], axis=0)
    out[:, before * width:] = jnp.transpose(last)


def on_pairs(amplitudes, tile_counts, tile_lists, integrals, n_vv, n_oo):
    tile_dev, slots, width, depth = integrals.shape
    rows = amplitudes.shape[1]
    tiles = n_vv * tile_dev
    before = tile_dev - 1
    place = jnp.stack([lax.axis_index("vv"), lax.axis_index("oo")]).astype(jnp.int32)

    far = shift(amplitudes, "oo", n_oo, 2)
    *arrays, amplitudes, table = cut(integrals, amplitudes, tile_lists, tile_counts)
    others = [shift(array, "oo", n_oo, 1) for array in arrays]
    block = pl.pallas_call(
        stack_kernel,
        out_shape=jax.ShapeDtypeStruct((2,) + amplitudes.shape, amplitudes.dtype),
        in_specs=[VMEM] * 2,
        out_specs=VMEM,
        compiler_params=pltpu.CompilerParams(vmem_limit_bytes=VMEM_BYTES),
        cost_estimate=pl.CostEstimate(flops=2**20, bytes_accessed=2**19, transcendentals=0),
    )(amplitudes, far)
    pieces, masks = [], []
    for mask in (0, 2, 4, 6):
        piece = shift(block, "vv", n_vv, mask) if mask else block
        pieces += [piece, shift(piece, "vv", n_vv, 1)]
        masks += [mask, mask ^ 1]
    scratch = [pltpu.SMEM(table.shape, table.dtype), pltpu.SemaphoreType.DMA]

    def call(kernel, out, n_smem, n_vmem, scratch, flops):
        return pl.pallas_call(
            kernel,
            out_shape=out,
            in_specs=[SMEM] * n_smem + [VMEM] * n_vmem,
            out_specs=jax.tree.map(lambda _: VMEM, out),
            scratch_shapes=scratch,
            compiler_params=pltpu.CompilerParams(vmem_limit_bytes=VMEM_BYTES),
            cost_estimate=pl.CostEstimate(flops=flops, bytes_accessed=2**21, transcendentals=0),
        )

    def f32(*shape):
        return jax.ShapeDtypeStruct(shape, jnp.float32)

    sums, last, stage = call(
        lambda *refs: own_kernel(masks, slots, *refs),
        (f32(before, 2 * rows, width), f32(width, 2 * rows), jax.ShapeDtypeStruct((2, tiles, rows, depth), far.dtype)),
        1, len(pieces) + 2 + PARTS, scratch, OWN_FLOPS,
    )(place, table, *pieces, *arrays)
    soon = before * rows * SOON // 8
    own, *away, table = call(
        lambda *refs: head_kernel(slots, *refs),
        (
            f32(before * rows, width), f32(soon, width), f32(before * rows - soon, width),
            jax.ShapeDtypeStruct(table.shape, table.dtype),
        ),
        1, 3, scratch, HEAD_FLOPS,
    )(place, stage, sums, others[0])
    picked = call(
        lambda *refs: pick_kernel(before, slots, *refs),
        jax.ShapeDtypeStruct((2 * rows, slots * depth), far.dtype),
        1, 2, scratch, 2**28,
    )(place, table, stage)
    soon, late = away
    late, picked = lax.optimization_barrier((late, picked))
    owns, gots = [own], [shift(x, "oo", n_oo, 2) for x in (soon, late)]
    for n in range(PARTS):
        own, away = call(
            lambda *refs, n=n: tail_kernel(slots, n, *refs), (f32(width // PARTS, rows),) * 2, 0, 3, [], 2**28
        )(last, picked, others[1 + n])
        owns.append(own)
        gots.append(shift(away, "oo", n_oo, 2))
    return call(join_kernel, f32(rows, tile_dev * width), 0, 3 + 2 * PARTS, [], 2**20)(*owns, *gots)


def on_device(amplitudes, tile_counts, tile_lists, integrals, n_vv, n_oo):
    if (n_vv, n_oo) == (8, 4):
        return on_pairs(amplitudes, tile_counts, tile_lists, integrals, n_vv, n_oo)
    slots = tile_lists.shape[1]
    live = jnp.clip(tile_counts - lax.axis_index("oo") * slots, 0, slots)
    rows = lax.all_gather(amplitudes, "oo", axis=0, tiled=False)
    everything = lax.all_gather(rows, "vv", axis=1, tiled=True)
    parts = plain_partials(tile_lists, live, everything, integrals)
    return lax.psum_scatter(parts.reshape(-1, parts.shape[2]), "oo", scatter_dimension=0, tiled=True)


def solution(mesh):
    n_vv, n_oo = mesh.shape["vv"], mesh.shape["oo"]
    placed = (P("vv", "oo", None), P("vv"), P("vv", "oo"), P("vv", "oo", None, None))
    return jax.shard_map(
        lambda *args: on_device(*args, n_vv, n_oo),
        mesh=mesh, in_specs=placed, out_specs=P("oo", "vv"), check_vma=False,
    )
```
